32 devices in a mesh: acq: 4 (over x, core), pulse: 8 (over z, y).
Axes of the slice: x: 2, y: 2, z: 4, core: 2. Of those that a mesh axis runs over, the one named last changes fastest.
Arguments:
- raw_echo: bfloat16 [4, 2, 8192, 1535], P('acq', None, 'pulse'), may hold values from -6 to 6
- chirp_phase: float32 [1024], replicated, may hold values from -3.140625 to 3.140625
- pulse_counts: int32 [4], P('acq'), may hold values from 4096 to 8192, as said below
- azimuth_rate: float32 [512], P('pulse'), may hold values from 0.25 to 1
- partner_bits: int32 [4, 2], P('acq'), may hold values from 0 to 1, as said below
Outputs:
- interfere_real: float32 [4, 2, 128, 512], P('acq', None, 'pulse')
- interfere_imag: float32 [4, 2, 128, 512], P('acq', None, 'pulse')
The draws below stay inside these ranges and needn't reach their ends.
Inputs may be any that keep to these rules, and one draw needn't show every extreme that they name: `pulse_counts`: at least half of 8192; some acquisition records all 8192 pulses and some exactly half. `partner_bits`: the two bits of a row differ.
All inputs are finite; a program needn't handle non-finite values.
Results may differ from the reference program's by a relative error of at most 0.0065.
Values may be sent and summed in bfloat16 or wider, within the bound.
A program may use at most 64 MiB of HBM per device.

```python
import math
import jax
import jax.numpy as jnp
from jax import lax

RNG = 512
TAPS = 1024
PULSES = 8192
LOOK_RNG = 4
LOOK_AZ = 16
ACQS = 4
ACQ_BITS = 2
ECHO = 1535


def draw_pulse_counts(key, part):
    first_key, second_key = jax.random.split(key)
    recorded = jax.random.randint(first_key, (ACQS,), PULSES // 2, PULSES + 1, dtype=jnp.int32)
    order = jax.random.permutation(second_key, ACQS)
    recorded = recorded.at[order[0]].set(PULSES)
    recorded = recorded.at[order[1]].set(PULSES // 2)
    return recorded.astype(jnp.int32)


def draw_partner_bits(key, part):
    first_key, second_key, third_key = jax.random.split(key, 3)
    leading = jax.random.randint(first_key, (ACQS,), 0, ACQ_BITS, dtype=jnp.int32)
    stride = jax.random.randint(second_key, (ACQS,), 1, ACQ_BITS, dtype=jnp.int32)
    trailing = (leading + stride) % ACQ_BITS
    chosen = jax.random.randint(third_key, (), 0, ACQS, dtype=jnp.int32)
    leading = leading.at[chosen].set(0)
    trailing = trailing.at[chosen].set(ACQ_BITS - 1)
    return jnp.stack([leading, trailing], axis=1).astype(jnp.int32)


def block_scale(own_key, dims, cuts, low, top_value):
    loudness, own = 1.0, jax.random.fold_in(own_key, 6)
    for axis_at, blocks in cuts:
        steps = jnp.exp(jax.random.uniform(jax.random.fold_in(own, axis_at), (blocks,), jnp.float32, low / len(cuts), top_value / len(cuts)))
        loudness = loudness * jnp.repeat(steps, dims[axis_at] // blocks).reshape([-1 if axis == axis_at else 1 for axis in range(len(dims))])
    return loudness


def scatter_about(own_key, dims, scale, most, shards=(), kind=jnp.bfloat16):
    array = jax.random.normal(own_key, dims, jnp.float32) * scale
    if len(shards) > 0:
        array = block_scale(own_key, dims, shards, -0.22, 0.18) * array
    return jnp.clip(array, min=-most, max=most).astype(kind)


def setup_inputs(seed: int = 0) -> dict:
    keys = jax.random.split(jax.random.key(seed), 6)
    return {
        "raw_echo": scatter_about(keys[0], (ACQS, 2, PULSES, ECHO), 1.0, 6.0, ((0, 4), (2, 8))),
        "chirp_phase": jnp.clip(jax.random.uniform(keys[1], (TAPS,), jnp.float32, -3.140625, 3.140625), -3.140625, 3.140625),
        "pulse_counts": draw_pulse_counts(jax.random.fold_in(keys[5], 71), 0),
        "azimuth_rate": jnp.clip(jnp.exp(math.log(1.0) - 1.3862944 * jax.random.uniform(keys[3], (RNG,), jnp.float32) ** block_scale(keys[3], (RNG,), ((0, 8),), -0.2, 0.2)), 0.25, 1.0),
        "partner_bits": draw_partner_bits(jax.random.fold_in(keys[5], 71), 0),
    }


def reference(raw_echo, chirp_phase, pulse_counts, azimuth_rate, partner_bits):
    amplitude = 2.0 / math.sqrt(TAPS)
    table_re = (amplitude * jnp.cos(chirp_phase)).astype(jnp.bfloat16).astype(jnp.float32)
    table_im = (amplitude * jnp.sin(chirp_phase)).astype(jnp.bfloat16).astype(jnp.float32)
    chirp = table_re + 1j * table_im
    span = RNG + TAPS
    chirp_spec = jnp.conj(jnp.fft.fft(chirp, n=span))
    freq_index = jnp.arange(PULSES, dtype=jnp.int32)
    signed = jnp.where(freq_index < PULSES // 2, freq_index, freq_index - PULSES).astype(jnp.float32)
    quad = signed * signed / PULSES
    phase = (jnp.pi * azimuth_rate)[:, None] * quad[None, :]
    matched = jnp.cos(phase) - 1j * jnp.sin(phase)
    pulse_index = jnp.arange(PULSES, dtype=jnp.int32)

    def focus(inputs):
        echoes, recorded = inputs
        signal = echoes[0].astype(jnp.float32) + 1j * echoes[1].astype(jnp.float32)
        spectrum = jnp.fft.fft(signal, n=span, axis=1)
        compressed = jnp.fft.ifft(spectrum * chirp_spec[None, :], axis=1)[:, :RNG]
        keep = (pulse_index < recorded).astype(jnp.float32)[:, None]
        comp_re = (jnp.real(compressed) * keep).astype(jnp.bfloat16).astype(jnp.float32)
        comp_im = (jnp.imag(compressed) * keep).astype(jnp.bfloat16).astype(jnp.float32)
        columns = (comp_re + 1j * comp_im).T
        focused = jnp.fft.ifft(jnp.fft.fft(columns, axis=1) * matched, axis=1)
        return jnp.stack([jnp.real(focused), jnp.imag(focused)]).astype(jnp.bfloat16)
    focused_all = lax.map(focus, (raw_echo, pulse_counts))
    acq_index = jnp.arange(ACQS, dtype=jnp.int32)

    def multilook(values):
        shaped = values.reshape(RNG // LOOK_RNG, LOOK_RNG, PULSES // LOOK_AZ, LOOK_AZ)
        return lax.optimization_barrier(jnp.mean(shaped, axis=(1, 3)))

    def interfere(inputs):
        number, chosen = inputs
        own_block = focused_all[number].astype(jnp.float32)
        real_parts = []
        imag_parts = []
        for slot in range(2):
            partner_index = jnp.bitwise_xor(number, jnp.left_shift(jnp.int32(1), chosen[slot]))
            partner = focused_all[partner_index].astype(jnp.float32)
            prod_re = own_block[0] * partner[0] + own_block[1] * partner[1]
            prod_im = own_block[1] * partner[0] - own_block[0] * partner[1]
            real_parts.append(multilook(prod_re))
            imag_parts.append(multilook(prod_im))
        return (jnp.stack(real_parts), jnp.stack(imag_parts))
    interfere_real, interfere_imag = lax.map(interfere, (acq_index, partner_bits))
    return (interfere_real, interfere_imag)
```

```python
import functools
import math

import jax
import jax.numpy as jnp
import numpy as np
from jax import lax
from jax.experimental import pallas as pl
from jax.experimental.pallas import tpu as pltpu
from jax.sharding import PartitionSpec as P

RNG = 512
TAPS = 1024
LOOK_RNG = 4
LOOK_AZ = 16


def partner_2(shard, axis, bit):
    return lax.ppermute(shard, axis, [(i, i ^ 1 << bit) for i in range(lax.axis_size(axis))])


def part_tables(length, inverse):
    steps = jnp.arange(length, dtype=jnp.int32)
    angle = 2.0 * jnp.pi * (steps[:, None] * steps[None, :] % length).astype(jnp.float32) / length
    cosine = jnp.cos(angle)
    sine = jnp.sin(angle)
    if inverse:
        sine = -sine
    return jnp.stack([jnp.stack([cosine, -sine]), jnp.stack([sine, cosine])])


def complex_product(left_re, left_im, right_re, right_im):
    return (left_re * right_re - left_im * right_im, left_re * right_im + left_im * right_re)


def compress(echoes, toeplitz, first_pulse, live_pulses, block_cols, window):
    pulse_rows = echoes.shape[1]
    parts_re = []
    parts_im = []
    for start in range(0, RNG, block_cols):
        segment = echoes[:, :, start : start + window]
        stacked = jnp.concatenate([segment[0], segment[1]], axis=1)
        result = lax.dot_general(
            toeplitz, stacked, (((1,), (1,)), ((), ())), preferred_element_type=jnp.float32
        )
        parts_re.append(result[:block_cols])
        parts_im.append(result[block_cols:])
    joined = jnp.stack([jnp.concatenate(parts_re, axis=0), jnp.concatenate(parts_im, axis=0)])
    pulse_ids = first_pulse + jnp.arange(pulse_rows, dtype=jnp.int32)
    keep = (pulse_ids < live_pulses).astype(jnp.float32)
    return (joined * keep[None, None, :]).astype(jnp.bfloat16)


def azimuth(turned, azimuth_rate):
    columns = turned.shape[1]
    length = turned.shape[2]
    outer_len = 64
    inner_len = length // outer_len
    highest = lax.Precision.HIGHEST
    signal = turned.astype(jnp.float32).reshape(2, columns, outer_len, inner_len)
    section_one = jnp.einsum(
        "pcab,pqak->qckb", signal, part_tables(outer_len, False), precision=highest
    )
    outer_ids = jnp.arange(outer_len, dtype=jnp.int32)
    inner_ids = jnp.arange(inner_len, dtype=jnp.int32)
    twist = (
        2.0
        * jnp.pi
        * (outer_ids[:, None] * inner_ids[None, :] % length).astype(jnp.float32)
        / length
    )
    twist_cos = jnp.cos(twist)
    twist_sin = jnp.sin(twist)
    turned_re, turned_im = complex_product(section_one[0], section_one[1], twist_cos, -twist_sin)
    spectrum = jnp.einsum(
        "pckb,pqbm->qckm",
        jnp.stack([turned_re, turned_im]),
        part_tables(inner_len, False),
        precision=highest,
    )
    freq_index = outer_ids[:, None] + outer_len * inner_ids[None, :]
    signed = jnp.where(freq_index < length // 2, freq_index, freq_index - length).astype(
        jnp.float32
    )
    quad = signed * signed / length
    phase = (jnp.pi * azimuth_rate)[:, None, None] * quad[None, :, :]
    filt_re, filt_im = complex_product(spectrum[0], spectrum[1], jnp.cos(phase), -jnp.sin(phase))
    back_one = jnp.einsum(
        "pckm,pqmb->qckb",
        jnp.stack([filt_re, filt_im]),
        part_tables(inner_len, True),
        precision=highest,
    )
    undo_re, undo_im = complex_product(back_one[0], back_one[1], twist_cos, twist_sin)
    restored = jnp.einsum(
        "pckb,pqka->qcab",
        jnp.stack([undo_re, undo_im]),
        part_tables(outer_len, True),
        precision=highest,
    )
    return (restored / length).reshape(2, columns, length)


def multilook(values):
    columns = values.shape[0]
    pulse_len = values.shape[1]
    shaped = values.reshape(columns // LOOK_RNG, LOOK_RNG, pulse_len // LOOK_AZ, LOOK_AZ)
    return jnp.mean(shaped, axis=(1, 3))


def cross_looks(own_block, partner):
    own_f = own_block.astype(jnp.float32)
    other_f = partner.astype(jnp.float32)
    prod_re = own_f[0] * other_f[0] + own_f[1] * other_f[1]
    prod_im = own_f[1] * other_f[0] - own_f[0] * other_f[1]
    return jnp.stack([multilook(prod_re), multilook(prod_im)])


def per_device(raw_echo, chirp_phase, pulse_counts, azimuth_rate, partner_bits):
    echoes = raw_echo[0]
    pulses_dev = echoes.shape[1]
    block_cols = min(256, RNG)
    window = block_cols + TAPS - 1
    amplitude = 2.0 / math.sqrt(TAPS)
    table_re = (amplitude * jnp.cos(chirp_phase)).astype(jnp.bfloat16)
    table_im = (amplitude * jnp.sin(chirp_phase)).astype(jnp.bfloat16)
    padding = jnp.zeros((block_cols,), jnp.bfloat16)
    band_re = jnp.tile(jnp.concatenate([table_re, padding]), block_cols)[
        : block_cols * window
    ].reshape(block_cols, window)
    band_im = jnp.tile(jnp.concatenate([table_im, padding]), block_cols)[
        : block_cols * window
    ].reshape(block_cols, window)
    toeplitz = jnp.concatenate(
        [jnp.concatenate([band_re, band_im], axis=1), jnp.concatenate([-band_im, band_re], axis=1)],
        axis=0,
    )
    live_pulses = pulse_counts[0]
    first_pulse = lax.axis_index("pulse") * pulses_dev
    compressed = compress(echoes, toeplitz, first_pulse, live_pulses, block_cols, window)
    turned = lax.all_to_all(compressed, "pulse", split_axis=1, concat_axis=2, tiled=True)
    focused = azimuth(turned, azimuth_rate).astype(jnp.bfloat16)
    chosen = partner_bits[0]
    bit_count = lax.axis_size("acq").bit_length() - 1
    arrived = [partner_2(focused, "acq", which) for which in range(bit_count)]
    results = []
    for slot in range(2):
        partner = arrived[0]
        for which in range(1, bit_count):
            partner = jnp.where(chosen[slot] == which, arrived[which], partner)
        results.append(cross_looks(focused, partner))
    interfere_real = jnp.stack([item[0] for item in results])[None]
    interfere_imag = jnp.stack([item[1] for item in results])[None]
    return (interfere_real, interfere_imag)


OUTER = 16


def butterflies(values, sign):
    count = len(values)
    if count == 1:
        return values
    even = butterflies(values[0::2], sign)
    odd = butterflies(values[1::2], sign)
    low, high = [], []
    for k in range(count // 2):
        e_re, e_im = even[k]
        o_re, o_im = odd[k]
        if k == 0:
            t_re, t_im = o_re, o_im
        elif 4 * k == count:
            t_re, t_im = (-o_im, o_re) if sign > 0 else (o_im, -o_re)
        else:
            c = math.cos(2.0 * math.pi * k / count)
            s = sign * math.sin(2.0 * math.pi * k / count)
            t_re, t_im = o_re * c - o_im * s, o_re * s + o_im * c
        low.append((e_re + t_re, e_im + t_im))
        high.append((e_re - t_re, e_im - t_im))
    return low + high


def compress_kernel(block_cols, counts_ref, phase_ref, echo_ref, out_ref, band):
    step = pl.program_id(0)
    pulses = echo_ref.shape[1]
    width = band.shape[2]
    window = block_cols + TAPS - 1

    @pl.when(step == 0)
    def _():
        amplitude = 2.0 / math.sqrt(TAPS)
        phase = phase_ref[...]
        for part, table in enumerate((jnp.cos(phase), jnp.sin(phase))):
            row = jnp.concatenate(
                [amplitude * table, jnp.zeros((1, width - TAPS), jnp.float32)], axis=1
            )
            rows = jnp.broadcast_to(row, (block_cols, width))
            band[part] = pltpu.roll(rows, 0, 1, stride=1, stride_axis=0).astype(jnp.bfloat16)

    first = counts_ref[1] + step * pulses
    ids = first + lax.broadcasted_iota(jnp.int32, (1, pulses), 1)
    keep = ids < counts_ref[0]
    band_re = band[0, :, :window]
    band_im = band[1, :, :window]
    dims = (((1,), (1,)), ((), ()))
    dot = functools.partial(
        lax.dot_general, dimension_numbers=dims, preferred_element_type=jnp.float32
    )
    per = out_ref.shape[2]
    slabs = block_cols // per
    for block in range(RNG // block_cols):
        lanes = pl.ds(block * block_cols, window)
        e_re = echo_ref[0, :, lanes]
        e_im = echo_ref[1, :, lanes]
        y_re = dot(band_re, e_re) + dot(band_im, e_im)
        y_im = dot(band_re, e_im) - dot(band_im, e_re)
        for part, y in enumerate((y_re, y_im)):
            kept = jnp.where(keep, y, 0.0).astype(jnp.bfloat16)
            out_ref[pl.ds(block * slabs, slabs), part] = kept.reshape(slabs, per, pulses)


def compress_call(echoes, phase, counts, devices):
    pulses = echoes.shape[1]
    step = min(256, pulses)
    block_cols = 256
    width = -(-(block_cols + TAPS - 1) // 128) * 128
    per = RNG // devices
    return pl.pallas_call(
        functools.partial(compress_kernel, block_cols),
        grid=(pulses // step,),
        out_shape=jax.ShapeDtypeStruct((devices, 2, per, pulses), jnp.bfloat16),
        in_specs=[
            pl.BlockSpec(memory_space=pltpu.SMEM),
            pl.BlockSpec((1, TAPS), lambda i: (0, 0)),
            pl.BlockSpec((2, step, echoes.shape[2]), lambda i: (0, i, 0)),
        ],
        out_specs=pl.BlockSpec((devices, 2, per, step), lambda i: (0, 0, 0, i)),
        scratch_shapes=[pltpu.VMEM((2, block_cols, width), jnp.bfloat16)],
        compiler_params=pltpu.CompilerParams(vmem_limit_bytes=48 * 2**20),
        name="compress",
    )(counts, phase, echoes)


def focus_kernel(
    acqs, pairs, x_ref, filt_ref, twist_ref, fwd_ref, inv_ref, pool_ref, look_ref, out_ref,
    held, image, prods,
):
    rows = x_ref.shape[2]
    local = x_ref.shape[3]
    inner = twist_ref.shape[2]
    per_src = local // inner
    chunk = 128

    def forward(index, carry):
        acq, at = index // (inner // chunk), index % (inner // chunk)
        values = []
        for a in range(OUTER):
            src = (a // per_src) * acqs + acq
            lane = pl.multiple_of((a % per_src) * inner + at * chunk, chunk)
            values.append(
                tuple(
                    x_ref[src, part, :, pl.ds(lane, chunk)].astype(jnp.float32)
                    for part in range(2)
                )
            )
        lane = pl.multiple_of(at * chunk, chunk)
        for k, (re, im) in enumerate(butterflies(values, -1)):
            c = twist_ref[0, pl.ds(k, 1), pl.ds(lane, chunk)]
            s = twist_ref[1, pl.ds(k, 1), pl.ds(lane, chunk)]
            held[acq, k, :, pl.ds(lane, chunk)] = (re * c + im * s).astype(jnp.bfloat16)
            lane_im = pl.multiple_of(lane + inner, chunk)
            held[acq, k, :, pl.ds(lane_im, chunk)] = (im * c - re * s).astype(jnp.bfloat16)
        return carry

    def middle(acq, carry):
        spec = jnp.dot(
            held[acq].reshape(OUTER * rows, 2 * inner),
            fwd_ref[...],
            preferred_element_type=jnp.float32,
        )
        s_re, s_im = spec[:, :inner], spec[:, inner:]
        f_re = filt_ref[0].reshape(OUTER * rows, inner)
        f_im = filt_ref[1].reshape(OUTER * rows, inner)
        m_re = (s_re * f_re - s_im * f_im).astype(jnp.bfloat16)
        m_im = (s_re * f_im + s_im * f_re).astype(jnp.bfloat16)
        back = jnp.dot(
            jnp.concatenate([m_re, m_im], axis=1), inv_ref[...],
            preferred_element_type=jnp.float32,
        )
        image[acq] = back.reshape(OUTER, rows, 2 * inner)
        return carry

    def inverse(index, carry):
        acq, at = index // (inner // chunk), index % (inner // chunk)
        lane = pl.multiple_of(at * chunk, chunk)
        lane_im = pl.multiple_of(lane + inner, chunk)
        values = []
        for k in range(OUTER):
            re = image[acq, k, :, pl.ds(lane, chunk)]
            im = image[acq, k, :, pl.ds(lane_im, chunk)]
            c = twist_ref[0, pl.ds(k, 1), pl.ds(lane, chunk)]
            s = twist_ref[1, pl.ds(k, 1), pl.ds(lane, chunk)]
            values.append((re * c - im * s, im * c + re * s))
        for a, (re, im) in enumerate(butterflies(values, 1)):
            image[acq, a, :, pl.ds(lane, chunk)] = re
            image[acq, a, :, pl.ds(lane_im, chunk)] = im
        return carry

    lax.fori_loop(0, acqs * (inner // chunk), forward, 0)
    lax.fori_loop(0, acqs, middle, 0)
    lax.fori_loop(0, acqs * (inner // chunk), inverse, 0)

    group = pool_ref.shape[0] // inner
    count = len(pairs) * rows
    parts = [[], []]
    for g in range(OUTER // group):
        for step in range(group):
            a = g * group + step
            lanes = pl.ds(step * inner, inner)
            for n, (one, two) in enumerate(pairs):
                o_re, o_im = image[one, a, :, :inner], image[one, a, :, inner:]
                t_re, t_im = image[two, a, :, :inner], image[two, a, :, inner:]
                for part, p in enumerate(
                    (o_re * t_re + o_im * t_im, o_im * t_re - o_re * t_im)
                ):
                    top = p.astype(jnp.bfloat16)
                    rest = (p - top.astype(jnp.float32)).astype(jnp.bfloat16)
                    at = part * count + n * rows
                    prods[pl.ds(at, rows), lanes] = top
                    prods[pl.ds(2 * count + at, rows), lanes] = rest
        z = jnp.dot(prods[...], pool_ref[...], preferred_element_type=jnp.float32)
        z = z[: 2 * count] + z[2 * count :]
        parts[0].append(z[:count])
        parts[1].append(z[count:])
    for part in range(2):
        out_ref[part] = jnp.dot(
            look_ref[part], jnp.concatenate(parts[part], axis=1),
            preferred_element_type=jnp.float32, precision=lax.Precision.HIGHEST,
        )


def focus_tables(acqs, rows, length):
    inner = length // OUTER
    b = np.arange(inner)
    angle = 2.0 * np.pi * (b[:, None] * b[None, :] % inner) / inner
    c, s = np.cos(angle), np.sin(angle)
    fwd = np.block([[c, -s], [s, c]]).astype(jnp.bfloat16)
    inv = np.block([[c, s], [-s, c]]).astype(jnp.bfloat16)
    angle = 2.0 * np.pi * (np.arange(OUTER)[:, None] * b[None, :]) / length
    twist = np.stack([np.cos(angle), np.sin(angle)]).astype(np.float32)
    span = 128 * LOOK_AZ
    pool = (np.arange(span)[:, None] // LOOK_AZ == np.arange(128)[None, :]).astype(jnp.bfloat16)
    bits = acqs.bit_length() - 1
    pairs = [(a, a ^ 1 << bit) for bit in range(bits) for a in range(acqs) if not a >> bit & 1]
    looks = rows // LOOK_RNG
    look = np.zeros((2, acqs, bits, looks, len(pairs), rows), np.float32)
    scale = 1.0 / (LOOK_RNG * LOOK_AZ)
    for n, (one, two) in enumerate(pairs):
        bit = (one ^ two).bit_length() - 1
        for r in range(rows):
            l = r // LOOK_RNG
            look[:, one, bit, l, n, r] = scale
            look[0, two, bit, l, n, r] = scale
            look[1, two, bit, l, n, r] = -scale
    look = look.reshape(2, acqs * bits * looks, len(pairs) * rows)
    return pairs, twist, fwd, inv, pool, look


def matched_filter(rate, length):
    inner = length // OUTER
    index = (
        jnp.arange(OUTER, dtype=jnp.int32)[:, None]
        + OUTER * jnp.arange(inner, dtype=jnp.int32)[None, :]
    )
    signed = jnp.where(index < length // 2, index, index - length).astype(jnp.float32)
    quad = signed * signed / length
    phase = (jnp.pi * rate)[None, :, None] * quad[:, None, :]
    return jnp.stack([jnp.cos(phase), -jnp.sin(phase)]) / length


def focus_call(x, filt, acqs):
    rows, local = x.shape[2], x.shape[3]
    length = x.shape[0] // acqs * local
    inner = length // OUTER
    pairs, twist, fwd, inv, pool, look = focus_tables(acqs, rows, length)
    return pl.pallas_call(
        functools.partial(focus_kernel, acqs, pairs),
        out_shape=jax.ShapeDtypeStruct((2, look.shape[1], length // LOOK_AZ), jnp.float32),
        in_specs=[pl.BlockSpec(memory_space=pltpu.VMEM)] * 7,
        out_specs=pl.BlockSpec(memory_space=pltpu.VMEM),
        scratch_shapes=[
            pltpu.VMEM((acqs, OUTER, rows, 2 * inner), jnp.bfloat16),
            pltpu.VMEM((acqs, OUTER, rows, 2 * inner), jnp.float32),
            pltpu.VMEM((4 * len(pairs) * rows, pool.shape[0]), jnp.bfloat16),
        ],
        compiler_params=pltpu.CompilerParams(vmem_limit_bytes=48 * 2**20),
        name="focus",
    )(x, filt, jnp.asarray(twist), jnp.asarray(fwd), jnp.asarray(inv), jnp.asarray(pool),
      jnp.asarray(look))


def per_device_joint(raw_echo, chirp_phase, pulse_counts, azimuth_rate, partner_bits):
    echoes = raw_echo[0]
    pulses_dev = echoes.shape[1]
    acqs, turns = lax.axis_size("acq"), lax.axis_size("pulse")
    bits = acqs.bit_length() - 1
    rows = RNG // (acqs * turns)
    looks = rows // LOOK_RNG
    first = lax.axis_index("pulse") * pulses_dev
    counts = jnp.stack([pulse_counts[0], first.astype(jnp.int32)])
    y = compress_call(echoes, chirp_phase[None], counts, acqs * turns)
    x = lax.all_to_all(y, ("pulse", "acq"), split_axis=0, concat_axis=0, tiled=True)
    rate = lax.dynamic_slice(azimuth_rate, (lax.axis_index("acq") * rows,), (rows,))
    filt = matched_filter(rate, pulses_dev * turns)
    out = focus_call(x, filt, acqs)
    cells = out.shape[2]
    out = out.reshape(2, acqs, bits * looks, cells)
    out = lax.all_to_all(out, "acq", split_axis=1, concat_axis=1, tiled=True)
    out = out.reshape(2, acqs, bits, looks, cells).transpose(0, 2, 1, 3, 4)
    out = out.reshape(2, bits, acqs * looks, cells)
    chosen = partner_bits[0]
    slots = []
    for slot in range(2):
        taken = out[:, 0]
        for which in range(1, bits):
            taken = jnp.where(chosen[slot] == which, out[:, which], taken)
        slots.append(taken)
    return (
        jnp.stack([item[0] for item in slots])[None],
        jnp.stack([item[1] for item in slots])[None],
    )


def solution(mesh):
    in_specs = (P("acq", None, "pulse", None), P(), P("acq"), P("pulse"), P("acq", None))
    out_specs = (P("acq", None, "pulse", None), P("acq", None, "pulse", None))
    devices = mesh.shape["acq"] * mesh.shape["pulse"]
    joint = RNG % (16 * devices) == 0
    return jax.shard_map(
        per_device_joint if joint else per_device,
        mesh=mesh, in_specs=in_specs, out_specs=out_specs, check_vma=False,
    )
```

```python
import functools
import math

import jax
import jax.numpy as jnp
import numpy as np
from jax import lax
from jax.experimental import pallas as pl
from jax.experimental.pallas import tpu as pltpu
from jax.sharding import PartitionSpec as P

RNG = 512
TAPS = 1024
LOOK_RNG = 4
LOOK_AZ = 16


def partner_2(shard, axis, bit):
    return lax.ppermute(shard, axis, [(i, i ^ 1 << bit) for i in range(lax.axis_size(axis))])


def part_tables(length, inverse):
    steps = jnp.arange(length, dtype=jnp.int32)
    angle = 2.0 * jnp.pi * (steps[:, None] * steps[None, :] % length).astype(jnp.float32) / length
    cosine = jnp.cos(angle)
    sine = jnp.sin(angle)
    if inverse:
        sine = -sine
    return jnp.stack([jnp.stack([cosine, -sine]), jnp.stack([sine, cosine])])


def complex_product(left_re, left_im, right_re, right_im):
    return (left_re * right_re - left_im * right_im, left_re * right_im + left_im * right_re)


def compress(echoes, toeplitz, first_pulse, live_pulses, block_cols, window):
    pulse_rows = echoes.shape[1]
    parts_re = []
    parts_im = []
    for start in range(0, RNG, block_cols):
        segment = echoes[:, :, start : start + window]
        stacked = jnp.concatenate([segment[0], segment[1]], axis=1)
        result = lax.dot_general(
            toeplitz, stacked, (((1,), (1,)), ((), ())), preferred_element_type=jnp.float32
        )
        parts_re.append(result[:block_cols])
        parts_im.append(result[block_cols:])
    joined = jnp.stack([jnp.concatenate(parts_re, axis=0), jnp.concatenate(parts_im, axis=0)])
    pulse_ids = first_pulse + jnp.arange(pulse_rows, dtype=jnp.int32)
    keep = (pulse_ids < live_pulses).astype(jnp.float32)
    return (joined * keep[None, None, :]).astype(jnp.bfloat16)


def azimuth(turned, azimuth_rate):
    columns = turned.shape[1]
    length = turned.shape[2]
    outer_len = 64
    inner_len = length // outer_len
    highest = lax.Precision.HIGHEST
    signal = turned.astype(jnp.float32).reshape(2, columns, outer_len, inner_len)
    section_one = jnp.einsum(
        "pcab,pqak->qckb", signal, part_tables(outer_len, False), precision=highest
    )
    outer_ids = jnp.arange(outer_len, dtype=jnp.int32)
    inner_ids = jnp.arange(inner_len, dtype=jnp.int32)
    twist = (
        2.0
        * jnp.pi
        * (outer_ids[:, None] * inner_ids[None, :] % length).astype(jnp.float32)
        / length
    )
    twist_cos = jnp.cos(twist)
    twist_sin = jnp.sin(twist)
    turned_re, turned_im = complex_product(section_one[0], section_one[1], twist_cos, -twist_sin)
    spectrum = jnp.einsum(
        "pckb,pqbm->qckm",
        jnp.stack([turned_re, turned_im]),
        part_tables(inner_len, False),
        precision=highest,
    )
    freq_index = outer_ids[:, None] + outer_len * inner_ids[None, :]
    signed = jnp.where(freq_index < length // 2, freq_index, freq_index - length).astype(
        jnp.float32
    )
    quad = signed * signed / length
    phase = (jnp.pi * azimuth_rate)[:, None, None] * quad[None, :, :]
    filt_re, filt_im = complex_product(spectrum[0], spectrum[1], jnp.cos(phase), -jnp.sin(phase))
    back_one = jnp.einsum(
        "pckm,pqmb->qckb",
        jnp.stack([filt_re, filt_im]),
        part_tables(inner_len, True),
        precision=highest,
    )
    undo_re, undo_im = complex_product(back_one[0], back_one[1], twist_cos, twist_sin)
    restored = jnp.einsum(
        "pckb,pqka->qcab",
        jnp.stack([undo_re, undo_im]),
        part_tables(outer_len, True),
        precision=highest,
    )
    return (restored / length).reshape(2, columns, length)


def multilook(values):
    columns = values.shape[0]
    pulse_len = values.shape[1]
    shaped = values.reshape(columns // LOOK_RNG, LOOK_RNG, pulse_len // LOOK_AZ, LOOK_AZ)
    return jnp.mean(shaped, axis=(1, 3))


def cross_looks(own_block, partner):
    own_f = own_block.astype(jnp.float32)
    other_f = partner.astype(jnp.float32)
    prod_re = own_f[0] * other_f[0] + own_f[1] * other_f[1]
    prod_im = own_f[1] * other_f[0] - own_f[0] * other_f[1]
    return jnp.stack([multilook(prod_re), multilook(prod_im)])


def per_device(raw_echo, chirp_phase, pulse_counts, azimuth_rate, partner_bits):
    echoes = raw_echo[0]
    pulses_dev = echoes.shape[1]
    block_cols = min(256, RNG)
    window = block_cols + TAPS - 1
    amplitude = 2.0 / math.sqrt(TAPS)
    table_re = (amplitude * jnp.cos(chirp_phase)).astype(jnp.bfloat16)
    table_im = (amplitude * jnp.sin(chirp_phase)).astype(jnp.bfloat16)
    padding = jnp.zeros((block_cols,), jnp.bfloat16)
    band_re = jnp.tile(jnp.concatenate([table_re, padding]), block_cols)[
        : block_cols * window
    ].reshape(block_cols, window)
    band_im = jnp.tile(jnp.concatenate([table_im, padding]), block_cols)[
        : block_cols * window
    ].reshape(block_cols, window)
    toeplitz = jnp.concatenate(
        [jnp.concatenate([band_re, band_im], axis=1), jnp.concatenate([-band_im, band_re], axis=1)],
        axis=0,
    )
    live_pulses = pulse_counts[0]
    first_pulse = lax.axis_index("pulse") * pulses_dev
    compressed = compress(echoes, toeplitz, first_pulse, live_pulses, block_cols, window)
    turned = lax.all_to_all(compressed, "pulse", split_axis=1, concat_axis=2, tiled=True)
    focused = azimuth(turned, azimuth_rate).astype(jnp.bfloat16)
    chosen = partner_bits[0]
    bit_count = lax.axis_size("acq").bit_length() - 1
    arrived = [partner_2(focused, "acq", which) for which in range(bit_count)]
    results = []
    for slot in range(2):
        partner = arrived[0]
        for which in range(1, bit_count):
            partner = jnp.where(chosen[slot] == which, arrived[which], partner)
        results.append(cross_looks(focused, partner))
    interfere_real = jnp.stack([item[0] for item in results])[None]
    interfere_imag = jnp.stack([item[1] for item in results])[None]
    return (interfere_real, interfere_imag)


OUTER = 16


def butterflies(values, sign):
    count = len(values)
    if count == 1:
        return values
    even = butterflies(values[0::2], sign)
    odd = butterflies(values[1::2], sign)
    low, high = [], []
    for k in range(count // 2):
        e_re, e_im = even[k]
        o_re, o_im = odd[k]
        if k == 0:
            t_re, t_im = o_re, o_im
        elif 4 * k == count:
            t_re, t_im = (-o_im, o_re) if sign > 0 else (o_im, -o_re)
        else:
            c = math.cos(2.0 * math.pi * k / count)
            s = sign * math.sin(2.0 * math.pi * k / count)
            t_re, t_im = o_re * c - o_im * s, o_re * s + o_im * c
        low.append((e_re + t_re, e_im + t_im))
        high.append((e_re - t_re, e_im - t_im))
    return low + high


def compress_kernel(block_cols, counts_ref, phase_ref, echo_ref, out_ref, band):
    step = pl.program_id(0)
    pulses = echo_ref.shape[2]
    width = band.shape[2]
    window = block_cols + TAPS - 1

    @pl.when(step == 0)
    def _():
        amplitude = 2.0 / math.sqrt(TAPS)
        phase = phase_ref[...]
        cosine, sine = amplitude * jnp.cos(phase), amplitude * jnp.sin(phase)
        even = lax.broadcasted_iota(jnp.int32, phase.shape, 1) % 2 == 0
        for part, table in enumerate(
            (jnp.where(even, cosine, sine), jnp.where(even, -sine, cosine))
        ):
            row = jnp.concatenate(
                [table, jnp.zeros((1, width - 2 * TAPS), jnp.float32)], axis=1
            )
            rows = jnp.broadcast_to(row, (block_cols, width))
            band[part] = pltpu.roll(rows, 0, 1, stride=2, stride_axis=0).astype(jnp.bfloat16)

    first = counts_ref[1] + step * pulses
    ids = first + lax.broadcasted_iota(jnp.int32, (1, pulses), 1)
    keep = ids < counts_ref[0]
    per = out_ref.shape[2]
    slabs = block_cols // per
    for block in range(RNG // block_cols):
        echo = echo_ref[pl.ds(block * block_cols, window)].reshape(2 * window, pulses)
        for part in range(2):
            y = jnp.dot(
                band[part, :, : 2 * window], echo, preferred_element_type=jnp.float32
            )
            kept = jnp.where(keep, y, 0.0).astype(jnp.bfloat16)
            out_ref[pl.ds(block * slabs, slabs), part] = kept.reshape(slabs, per, pulses)


def compress_call(echoes, phase, counts, devices):
    pulses = echoes.shape[2]
    step = min(256, pulses)
    block_cols = 256
    width = -(-2 * (block_cols + TAPS - 1) // 128) * 128
    per = RNG // devices
    return pl.pallas_call(
        functools.partial(compress_kernel, block_cols),
        grid=(pulses // step,),
        out_shape=jax.ShapeDtypeStruct((devices, 2, per, pulses), jnp.bfloat16),
        in_specs=[
            pl.BlockSpec(memory_space=pltpu.SMEM),
            pl.BlockSpec((1, 2 * TAPS), lambda i: (0, 0)),
            pl.BlockSpec((echoes.shape[0], 2, step), lambda i: (0, 0, i)),
        ],
        out_specs=pl.BlockSpec((devices, 2, per, step), lambda i: (0, 0, 0, i)),
        scratch_shapes=[pltpu.VMEM((2, block_cols, width), jnp.bfloat16)],
        compiler_params=pltpu.CompilerParams(vmem_limit_bytes=48 * 2**20),
        name="compress",
    )(counts, phase, echoes)


def focus_kernel(
    acqs, pairs, x_ref, filt_ref, twist_ref, fwd_ref, inv_ref, pool_ref, look_ref, out_ref,
    held, image, prods,
):
    rows = x_ref.shape[2]
    local = x_ref.shape[3]
    inner = twist_ref.shape[2]
    per_src = local // inner
    chunk = 128

    def forward(index, carry):
        acq, at = index // (inner // chunk), index % (inner // chunk)
        values = []
        for a in range(OUTER):
            src = (a // per_src) * acqs + acq
            lane = pl.multiple_of((a % per_src) * inner + at * chunk, chunk)
            values.append(
                tuple(
                    x_ref[src, part, :, pl.ds(lane, chunk)].astype(jnp.float32)
                    for part in range(2)
                )
            )
        lane = pl.multiple_of(at * chunk, chunk)
        for k, (re, im) in enumerate(butterflies(values, -1)):
            c = twist_ref[0, pl.ds(k, 1), pl.ds(lane, chunk)]
            s = twist_ref[1, pl.ds(k, 1), pl.ds(lane, chunk)]
            held[acq, k, :, pl.ds(lane, chunk)] = (re * c + im * s).astype(jnp.bfloat16)
            lane_im = pl.multiple_of(lane + inner, chunk)
            held[acq, k, :, pl.ds(lane_im, chunk)] = (im * c - re * s).astype(jnp.bfloat16)
        return carry

    def middle(acq, carry):
        spec = jnp.dot(
            held[acq].reshape(OUTER * rows, 2 * inner),
            fwd_ref[...],
            preferred_element_type=jnp.float32,
        )
        s_re, s_im = spec[:, :inner], spec[:, inner:]
        f_re = filt_ref[0].reshape(OUTER * rows, inner)
        f_im = filt_ref[1].reshape(OUTER * rows, inner)
        m_re = (s_re * f_re - s_im * f_im).astype(jnp.bfloat16)
        m_im = (s_re * f_im + s_im * f_re).astype(jnp.bfloat16)
        back = jnp.dot(
            jnp.concatenate([m_re, m_im], axis=1), inv_ref[...],
            preferred_element_type=jnp.float32,
        )
        image[acq] = back.reshape(OUTER, rows, 2 * inner)
        return carry

    def inverse(index, carry):
        acq, at = index // (inner // chunk), index % (inner // chunk)
        lane = pl.multiple_of(at * chunk, chunk)
        lane_im = pl.multiple_of(lane + inner, chunk)
        values = []
        for k in range(OUTER):
            re = image[acq, k, :, pl.ds(lane, chunk)]
            im = image[acq, k, :, pl.ds(lane_im, chunk)]
            c = twist_ref[0, pl.ds(k, 1), pl.ds(lane, chunk)]
            s = twist_ref[1, pl.ds(k, 1), pl.ds(lane, chunk)]
            values.append((re * c - im * s, im * c + re * s))
        for a, (re, im) in enumerate(butterflies(values, 1)):
            image[acq, a, :, pl.ds(lane, chunk)] = re
            image[acq, a, :, pl.ds(lane_im, chunk)] = im
        return carry

    lax.fori_loop(0, acqs * (inner // chunk), forward, 0)
    lax.fori_loop(0, acqs, middle, 0)
    lax.fori_loop(0, acqs * (inner // chunk), inverse, 0)

    group = pool_ref.shape[0] // inner
    count = len(pairs) * rows
    parts = [[], []]
    for g in range(OUTER // group):
        for step in range(group):
            a = g * group + step
            lanes = pl.ds(step * inner, inner)
            for n, (one, two) in enumerate(pairs):
                o_re, o_im = image[one, a, :, :inner], image[one, a, :, inner:]
                t_re, t_im = image[two, a, :, :inner], image[two, a, :, inner:]
                for part, p in enumerate(
                    (o_re * t_re + o_im * t_im, o_im * t_re - o_re * t_im)
                ):
                    top = p.astype(jnp.bfloat16)
                    rest = (p - top.astype(jnp.float32)).astype(jnp.bfloat16)
                    at = part * count + n * rows
                    prods[pl.ds(at, rows), lanes] = top
                    prods[pl.ds(2 * count + at, rows), lanes] = rest
        z = jnp.dot(prods[...], pool_ref[...], preferred_element_type=jnp.float32)
        z = z[: 2 * count] + z[2 * count :]
        parts[0].append(z[:count])
        parts[1].append(z[count:])
    for part in range(2):
        out_ref[part] = jnp.dot(
            look_ref[part], jnp.concatenate(parts[part], axis=1),
            preferred_element_type=jnp.float32, precision=lax.Precision.HIGHEST,
        )


def focus_tables(acqs, rows, length):
    inner = length // OUTER
    b = np.arange(inner)
    angle = 2.0 * np.pi * (b[:, None] * b[None, :] % inner) / inner
    c, s = np.cos(angle), np.sin(angle)
    fwd = np.block([[c, -s], [s, c]]).astype(jnp.bfloat16)
    inv = np.block([[c, s], [-s, c]]).astype(jnp.bfloat16)
    angle = 2.0 * np.pi * (np.arange(OUTER)[:, None] * b[None, :]) / length
    twist = np.stack([np.cos(angle), np.sin(angle)]).astype(np.float32)
    span = 128 * LOOK_AZ
    pool = (np.arange(span)[:, None] // LOOK_AZ == np.arange(128)[None, :]).astype(jnp.bfloat16)
    bits = acqs.bit_length() - 1
    pairs = [(a, a ^ 1 << bit) for bit in range(bits) for a in range(acqs) if not a >> bit & 1]
    looks = rows // LOOK_RNG
    look = np.zeros((2, acqs, bits, looks, len(pairs), rows), np.float32)
    scale = 1.0 / (LOOK_RNG * LOOK_AZ)
    for n, (one, two) in enumerate(pairs):
        bit = (one ^ two).bit_length() - 1
        for r in range(rows):
            l = r // LOOK_RNG
            look[:, one, bit, l, n, r] = scale
            look[0, two, bit, l, n, r] = scale
            look[1, two, bit, l, n, r] = -scale
    look = look.reshape(2, acqs * bits * looks, len(pairs) * rows)
    return pairs, twist, fwd, inv, pool, look


def matched_filter(rate, length):
    inner = length // OUTER
    index = (
        jnp.arange(OUTER, dtype=jnp.int32)[:, None]
        + OUTER * jnp.arange(inner, dtype=jnp.int32)[None, :]
    )
    signed = jnp.where(index < length // 2, index, index - length).astype(jnp.float32)
    quad = signed * signed / length
    phase = (jnp.pi * rate)[None, :, None] * quad[:, None, :]
    return jnp.stack([jnp.cos(phase), -jnp.sin(phase)]) / length


def focus_call(x, filt, acqs):
    rows, local = x.shape[2], x.shape[3]
    length = x.shape[0] // acqs * local
    inner = length // OUTER
    pairs, twist, fwd, inv, pool, look = focus_tables(acqs, rows, length)
    return pl.pallas_call(
        functools.partial(focus_kernel, acqs, pairs),
        out_shape=jax.ShapeDtypeStruct((2, look.shape[1], length // LOOK_AZ), jnp.float32),
        in_specs=[pl.BlockSpec(memory_space=pltpu.VMEM)] * 7,
        out_specs=pl.BlockSpec(memory_space=pltpu.VMEM),
        scratch_shapes=[
            pltpu.VMEM((acqs, OUTER, rows, 2 * inner), jnp.bfloat16),
            pltpu.VMEM((acqs, OUTER, rows, 2 * inner), jnp.float32),
            pltpu.VMEM((4 * len(pairs) * rows, pool.shape[0]), jnp.bfloat16),
        ],
        compiler_params=pltpu.CompilerParams(vmem_limit_bytes=48 * 2**20),
        name="focus",
    )(x, filt, jnp.asarray(twist), jnp.asarray(fwd), jnp.asarray(inv), jnp.asarray(pool),
      jnp.asarray(look))


def per_device_joint(raw_echo, chirp_phase, pulse_counts, azimuth_rate, partner_bits):
    echoes = raw_echo[0].transpose(2, 0, 1)
    pulses_dev = echoes.shape[2]
    acqs, turns = lax.axis_size("acq"), lax.axis_size("pulse")
    bits = acqs.bit_length() - 1
    rows = RNG // (acqs * turns)
    looks = rows // LOOK_RNG
    first = lax.axis_index("pulse") * pulses_dev
    counts = jnp.stack([pulse_counts[0], first.astype(jnp.int32)])
    y = compress_call(echoes, jnp.repeat(chirp_phase, 2)[None], counts, acqs * turns)
    x = lax.all_to_all(y, ("pulse", "acq"), split_axis=0, concat_axis=0, tiled=True)
    rate = lax.dynamic_slice(azimuth_rate, (lax.axis_index("acq") * rows,), (rows,))
    filt = matched_filter(rate, pulses_dev * turns)
    out = focus_call(x, filt, acqs)
    cells = out.shape[2]
    out = out.reshape(2, acqs, bits * looks, cells)
    out = lax.all_to_all(out, "acq", split_axis=1, concat_axis=1, tiled=True)
    out = out.reshape(2, acqs, bits, looks, cells).transpose(0, 2, 1, 3, 4)
    out = out.reshape(2, bits, acqs * looks, cells)
    chosen = partner_bits[0]
    slots = []
    for slot in range(2):
        taken = out[:, 0]
        for which in range(1, bits):
            taken = jnp.where(chosen[slot] == which, out[:, which], taken)
        slots.append(taken)
    return (
        jnp.stack([item[0] for item in slots])[None],
        jnp.stack([item[1] for item in slots])[None],
    )


def solution(mesh):
    in_specs = (P("acq", None, "pulse", None), P(), P("acq"), P("pulse"), P("acq", None))
    out_specs = (P("acq", None, "pulse", None), P("acq", None, "pulse", None))
    devices = mesh.shape["acq"] * mesh.shape["pulse"]
    joint = RNG % (16 * devices) == 0
    return jax.shard_map(
        per_device_joint if joint else per_device,
        mesh=mesh, in_specs=in_specs, out_specs=out_specs, check_vma=False,
    )
```

```python
import functools
import math

import jax
import jax.numpy as jnp
import numpy as np
from jax import lax
from jax.experimental import pallas as pl
from jax.experimental.pallas import tpu as pltpu
from jax.sharding import PartitionSpec as P

RNG = 512
TAPS = 1024
LOOK_RNG = 4
LOOK_AZ = 16


def partner_2(shard, axis, bit):
    return lax.ppermute(shard, axis, [(i, i ^ 1 << bit) for i in range(lax.axis_size(axis))])


def part_tables(length, inverse):
    steps = jnp.arange(length, dtype=jnp.int32)
    angle = 2.0 * jnp.pi * (steps[:, None] * steps[None, :] % length).astype(jnp.float32) / length
    cosine = jnp.cos(angle)
    sine = jnp.sin(angle)
    if inverse:
        sine = -sine
    return jnp.stack([jnp.stack([cosine, -sine]), jnp.stack([sine, cosine])])


def complex_product(left_re, left_im, right_re, right_im):
    return (left_re * right_re - left_im * right_im, left_re * right_im + left_im * right_re)


def compress(echoes, toeplitz, first_pulse, live_pulses, block_cols, window):
    pulse_rows = echoes.shape[1]
    parts_re = []
    parts_im = []
    for start in range(0, RNG, block_cols):
        segment = echoes[:, :, start : start + window]
        stacked = jnp.concatenate([segment[0], segment[1]], axis=1)
        result = lax.dot_general(
            toeplitz, stacked, (((1,), (1,)), ((), ())), preferred_element_type=jnp.float32
        )
        parts_re.append(result[:block_cols])
        parts_im.append(result[block_cols:])
    joined = jnp.stack([jnp.concatenate(parts_re, axis=0), jnp.concatenate(parts_im, axis=0)])
    pulse_ids = first_pulse + jnp.arange(pulse_rows, dtype=jnp.int32)
    keep = (pulse_ids < live_pulses).astype(jnp.float32)
    return (joined * keep[None, None, :]).astype(jnp.bfloat16)


def azimuth(turned, azimuth_rate):
    columns = turned.shape[1]
    length = turned.shape[2]
    outer_len = 64
    inner_len = length // outer_len
    highest = lax.Precision.HIGHEST
    signal = turned.astype(jnp.float32).reshape(2, columns, outer_len, inner_len)
    section_one = jnp.einsum(
        "pcab,pqak->qckb", signal, part_tables(outer_len, False), precision=highest
    )
    outer_ids = jnp.arange(outer_len, dtype=jnp.int32)
    inner_ids = jnp.arange(inner_len, dtype=jnp.int32)
    twist = (
        2.0
        * jnp.pi
        * (outer_ids[:, None] * inner_ids[None, :] % length).astype(jnp.float32)
        / length
    )
    twist_cos = jnp.cos(twist)
    twist_sin = jnp.sin(twist)
    turned_re, turned_im = complex_product(section_one[0], section_one[1], twist_cos, -twist_sin)
    spectrum = jnp.einsum(
        "pckb,pqbm->qckm",
        jnp.stack([turned_re, turned_im]),
        part_tables(inner_len, False),
        precision=highest,
    )
    freq_index = outer_ids[:, None] + outer_len * inner_ids[None, :]
    signed = jnp.where(freq_index < length // 2, freq_index, freq_index - length).astype(
        jnp.float32
    )
    quad = signed * signed / length
    phase = (jnp.pi * azimuth_rate)[:, None, None] * quad[None, :, :]
    filt_re, filt_im = complex_product(spectrum[0], spectrum[1], jnp.cos(phase), -jnp.sin(phase))
    back_one = jnp.einsum(
        "pckm,pqmb->qckb",
        jnp.stack([filt_re, filt_im]),
        part_tables(inner_len, True),
        precision=highest,
    )
    undo_re, undo_im = complex_product(back_one[0], back_one[1], twist_cos, twist_sin)
    restored = jnp.einsum(
        "pckb,pqka->qcab",
        jnp.stack([undo_re, undo_im]),
        part_tables(outer_len, True),
        precision=highest,
    )
    return (restored / length).reshape(2, columns, length)


def multilook(values):
    columns = values.shape[0]
    pulse_len = values.shape[1]
    shaped = values.reshape(columns // LOOK_RNG, LOOK_RNG, pulse_len // LOOK_AZ, LOOK_AZ)
    return jnp.mean(shaped, axis=(1, 3))


def cross_looks(own_block, partner):
    own_f = own_block.astype(jnp.float32)
    other_f = partner.astype(jnp.float32)
    prod_re = own_f[0] * other_f[0] + own_f[1] * other_f[1]
    prod_im = own_f[1] * other_f[0] - own_f[0] * other_f[1]
    return jnp.stack([multilook(prod_re), multilook(prod_im)])


def per_device(raw_echo, chirp_phase, pulse_counts, azimuth_rate, partner_bits):
    echoes = raw_echo[0]
    pulses_dev = echoes.shape[1]
    block_cols = min(256, RNG)
    window = block_cols + TAPS - 1
    amplitude = 2.0 / math.sqrt(TAPS)
    table_re = (amplitude * jnp.cos(chirp_phase)).astype(jnp.bfloat16)
    table_im = (amplitude * jnp.sin(chirp_phase)).astype(jnp.bfloat16)
    padding = jnp.zeros((block_cols,), jnp.bfloat16)
    band_re = jnp.tile(jnp.concatenate([table_re, padding]), block_cols)[
        : block_cols * window
    ].reshape(block_cols, window)
    band_im = jnp.tile(jnp.concatenate([table_im, padding]), block_cols)[
        : block_cols * window
    ].reshape(block_cols, window)
    toeplitz = jnp.concatenate(
        [jnp.concatenate([band_re, band_im], axis=1), jnp.concatenate([-band_im, band_re], axis=1)],
        axis=0,
    )
    live_pulses = pulse_counts[0]
    first_pulse = lax.axis_index("pulse") * pulses_dev
    compressed = compress(echoes, toeplitz, first_pulse, live_pulses, block_cols, window)
    turned = lax.all_to_all(compressed, "pulse", split_axis=1, concat_axis=2, tiled=True)
    focused = azimuth(turned, azimuth_rate).astype(jnp.bfloat16)
    chosen = partner_bits[0]
    bit_count = lax.axis_size("acq").bit_length() - 1
    arrived = [partner_2(focused, "acq", which) for which in range(bit_count)]
    results = []
    for slot in range(2):
        partner = arrived[0]
        for which in range(1, bit_count):
            partner = jnp.where(chosen[slot] == which, arrived[which], partner)
        results.append(cross_looks(focused, partner))
    interfere_real = jnp.stack([item[0] for item in results])[None]
    interfere_imag = jnp.stack([item[1] for item in results])[None]
    return (interfere_real, interfere_imag)


OUTER = 16


def butterflies(values, sign):
    count = len(values)
    if count == 1:
        return values
    even = butterflies(values[0::2], sign)
    odd = butterflies(values[1::2], sign)
    low, high = [], []
    for k in range(count // 2):
        e_re, e_im = even[k]
        o_re, o_im = odd[k]
        if k == 0:
            t_re, t_im = o_re, o_im
        elif 4 * k == count:
            t_re, t_im = (-o_im, o_re) if sign > 0 else (o_im, -o_re)
        else:
            c = math.cos(2.0 * math.pi * k / count)
            s = sign * math.sin(2.0 * math.pi * k / count)
            t_re, t_im = o_re * c - o_im * s, o_re * s + o_im * c
        low.append((e_re + t_re, e_im + t_im))
        high.append((e_re - t_re, e_im - t_im))
    return low + high


def compress_kernel(
    block_cols, counts_ref, phase_ref, echo_ref, turned_ref, band, ready, send_sem, recv_sem,
    own_sem,
):
    step = pl.program_id(0)
    steps = pl.num_programs(0)
    acqs = lax.axis_size("acq")
    devices = acqs * lax.axis_size("pulse")
    me = lax.axis_index("pulse") * acqs + lax.axis_index("acq")
    barrier = pltpu.get_barrier_semaphore()

    def place(d):
        peer = me ^ d
        return peer, (peer % acqs, peer // acqs)

    @pl.when(step == 0)
    def _():
        def greet(d, carry):
            pl.semaphore_signal(
                barrier, inc=1, device_id=place(d)[1], device_id_type=pl.DeviceIdType.MESH
            )
            return carry

        lax.fori_loop(1, devices, greet, 0)

    pulses = echo_ref.shape[2]
    width = band.shape[2]
    window = block_cols + TAPS - 1

    @pl.when(step == 0)
    def _():
        amplitude = 2.0 / math.sqrt(TAPS)
        phase = phase_ref[...]
        cosine, sine = amplitude * jnp.cos(phase), amplitude * jnp.sin(phase)
        even = lax.broadcasted_iota(jnp.int32, phase.shape, 1) % 2 == 0
        for part, table in enumerate(
            (jnp.where(even, cosine, sine), jnp.where(even, -sine, cosine))
        ):
            row = jnp.concatenate(
                [table, jnp.zeros((1, width - 2 * TAPS), jnp.float32)], axis=1
            )
            rows = jnp.broadcast_to(row, (block_cols, width))
            band[part] = pltpu.roll(rows, 0, 1, stride=2, stride_axis=0).astype(jnp.bfloat16)

    first = counts_ref[1] + step * pulses
    ids = first + lax.broadcasted_iota(jnp.int32, (1, pulses), 1)
    keep = ids < counts_ref[0]
    per = ready.shape[3]
    slabs = block_cols // per
    for block in range(RNG // block_cols):
        echo = echo_ref[pl.ds(block * block_cols, window)].reshape(2 * window, pulses)
        for part in range(2):
            y = jnp.dot(
                band[part, :, : 2 * window], echo, preferred_element_type=jnp.float32
            )
            kept = jnp.where(keep, y, 0.0).astype(jnp.bfloat16)
            ready[step, pl.ds(block * slabs, slabs), part] = kept.reshape(slabs, per, pulses)

    @pl.when(step == 0)
    def _():
        pl.semaphore_wait(barrier, devices - 1)

    def remote(at, d):
        peer, where = place(d)
        lanes = pl.ds(pl.multiple_of(at * pulses, 128), pulses)
        return pltpu.make_async_remote_copy(
            src_ref=ready.at[at, peer],
            dst_ref=turned_ref.at[me, :, :, lanes],
            send_sem=send_sem.at[at, d],
            recv_sem=recv_sem.at[at, d],
            device_id=where,
            device_id_type=pl.DeviceIdType.MESH,
        )

    def own(at):
        lanes = pl.ds(pl.multiple_of(at * pulses, 128), pulses)
        return pltpu.make_async_copy(
            ready.at[at, me], turned_ref.at[me, :, :, lanes], own_sem.at[at]
        )

    half = devices // 2

    def send(i, carry):
        remote(step, devices - 1 - i).start()
        remote(step, half - 1 - i).start()
        return carry

    lax.fori_loop(0, half - 1, send, 0)
    remote(step, half).start()
    own(step).start()

    @pl.when(step == steps - 1)
    def _():
        def finish(i, carry):
            remote(i // (devices - 1), i % (devices - 1) + 1).wait()
            return carry

        lax.fori_loop(0, steps * (devices - 1), finish, 0)
        for at in range(ready.shape[0]):
            own(at).wait()


def compress_call(echoes, phase, counts, devices):
    pulses = echoes.shape[2]
    step = min(512, pulses)
    steps = pulses // step
    block_cols = 256
    width = -(-2 * (block_cols + TAPS - 1) // 128) * 128
    per = RNG // devices
    return pl.pallas_call(
        functools.partial(compress_kernel, block_cols),
        grid=(steps,),
        out_shape=jax.ShapeDtypeStruct((devices, 2, per, pulses), jnp.bfloat16),
        in_specs=[
            pl.BlockSpec(memory_space=pltpu.SMEM),
            pl.BlockSpec((1, 2 * TAPS), lambda i: (0, 0)),
            pl.BlockSpec((echoes.shape[0], 2, step), lambda i: (0, 0, i)),
        ],
        out_specs=pl.BlockSpec(memory_space=pl.ANY),
        scratch_shapes=[
            pltpu.VMEM((2, block_cols, width), jnp.bfloat16),
            pltpu.VMEM((steps, devices, 2, per, step), jnp.bfloat16),
            pltpu.SemaphoreType.DMA((steps, devices)),
            pltpu.SemaphoreType.DMA((steps, devices)),
            pltpu.SemaphoreType.DMA((steps,)),
        ],
        compiler_params=pltpu.CompilerParams(
            vmem_limit_bytes=40 * 2**20, collective_id=0, has_side_effects=True
        ),
        name="compress",
    )(counts, phase, echoes)


def focus_kernel(
    acqs, pairs, x_ref, filt_ref, twist_ref, fwd_ref, inv_ref, pool_ref, look_ref, out_ref,
    held, image, prods,
):
    rows = x_ref.shape[2]
    local = x_ref.shape[3]
    inner = twist_ref.shape[2]
    per_src = local // inner
    chunk = 128

    def forward(index, carry):
        acq, at = index // (inner // chunk), index % (inner // chunk)
        values = []
        for a in range(OUTER):
            src = (a // per_src) * acqs + acq
            lane = pl.multiple_of((a % per_src) * inner + at * chunk, chunk)
            values.append(
                tuple(
                    x_ref[src, part, :, pl.ds(lane, chunk)].astype(jnp.float32)
                    for part in range(2)
                )
            )
        lane = pl.multiple_of(at * chunk, chunk)
        for k, (re, im) in enumerate(butterflies(values, -1)):
            c = twist_ref[0, pl.ds(k, 1), pl.ds(lane, chunk)]
            s = twist_ref[1, pl.ds(k, 1), pl.ds(lane, chunk)]
            held[acq, k, :, pl.ds(lane, chunk)] = (re * c + im * s).astype(jnp.bfloat16)
            lane_im = pl.multiple_of(lane + inner, chunk)
            held[acq, k, :, pl.ds(lane_im, chunk)] = (im * c - re * s).astype(jnp.bfloat16)
        return carry

    def middle(acq, carry):
        spec = jnp.dot(
            held[acq].reshape(OUTER * rows, 2 * inner),
            fwd_ref[...],
            preferred_element_type=jnp.float32,
        )
        s_re, s_im = spec[:, :inner], spec[:, inner:]
        f_re = filt_ref[0].reshape(OUTER * rows, inner)
        f_im = filt_ref[1].reshape(OUTER * rows, inner)
        m_re = (s_re * f_re - s_im * f_im).astype(jnp.bfloat16)
        m_im = (s_re * f_im + s_im * f_re).astype(jnp.bfloat16)
        back = jnp.dot(
            jnp.concatenate([m_re, m_im], axis=1), inv_ref[...],
            preferred_element_type=jnp.float32,
        )
        image[acq] = back.reshape(OUTER, rows, 2 * inner)
        return carry

    def inverse(index, carry):
        acq, at = index // (inner // chunk), index % (inner // chunk)
        lane = pl.multiple_of(at * chunk, chunk)
        lane_im = pl.multiple_of(lane + inner, chunk)
        values = []
        for k in range(OUTER):
            re = image[acq, k, :, pl.ds(lane, chunk)]
            im = image[acq, k, :, pl.ds(lane_im, chunk)]
            c = twist_ref[0, pl.ds(k, 1), pl.ds(lane, chunk)]
            s = twist_ref[1, pl.ds(k, 1), pl.ds(lane, chunk)]
            values.append((re * c - im * s, im * c + re * s))
        for a, (re, im) in enumerate(butterflies(values, 1)):
            image[acq, a, :, pl.ds(lane, chunk)] = re
            image[acq, a, :, pl.ds(lane_im, chunk)] = im
        return carry

    lax.fori_loop(0, acqs * (inner // chunk), forward, 0)
    lax.fori_loop(0, acqs, middle, 0)
    lax.fori_loop(0, acqs * (inner // chunk), inverse, 0)

    group = pool_ref.shape[0] // inner
    count = len(pairs) * rows
    parts = [[], []]
    for g in range(OUTER // group):
        for step in range(group):
            a = g * group + step
            lanes = pl.ds(step * inner, inner)
            for n, (one, two) in enumerate(pairs):
                o_re, o_im = image[one, a, :, :inner], image[one, a, :, inner:]
                t_re, t_im = image[two, a, :, :inner], image[two, a, :, inner:]
                for part, p in enumerate(
                    (o_re * t_re + o_im * t_im, o_im * t_re - o_re * t_im)
                ):
                    top = p.astype(jnp.bfloat16)
                    rest = (p - top.astype(jnp.float32)).astype(jnp.bfloat16)
                    at = part * count + n * rows
                    prods[pl.ds(at, rows), lanes] = top
                    prods[pl.ds(2 * count + at, rows), lanes] = rest
        z = jnp.dot(prods[...], pool_ref[...], preferred_element_type=jnp.float32)
        z = z[: 2 * count] + z[2 * count :]
        parts[0].append(z[:count])
        parts[1].append(z[count:])
    for part in range(2):
        out_ref[part] = jnp.dot(
            look_ref[part], jnp.concatenate(parts[part], axis=1),
            preferred_element_type=jnp.float32, precision=lax.Precision.HIGHEST,
        )


def focus_tables(acqs, rows, length):
    inner = length // OUTER
    b = np.arange(inner)
    angle = 2.0 * np.pi * (b[:, None] * b[None, :] % inner) / inner
    c, s = np.cos(angle), np.sin(angle)
    fwd = np.block([[c, -s], [s, c]]).astype(jnp.bfloat16)
    inv = np.block([[c, s], [-s, c]]).astype(jnp.bfloat16)
    angle = 2.0 * np.pi * (np.arange(OUTER)[:, None] * b[None, :]) / length
    twist = np.stack([np.cos(angle), np.sin(angle)]).astype(np.float32)
    span = 128 * LOOK_AZ
    pool = (np.arange(span)[:, None] // LOOK_AZ == np.arange(128)[None, :]).astype(jnp.bfloat16)
    bits = acqs.bit_length() - 1
    pairs = [(a, a ^ 1 << bit) for bit in range(bits) for a in range(acqs) if not a >> bit & 1]
    looks = rows // LOOK_RNG
    look = np.zeros((2, acqs, bits, looks, len(pairs), rows), np.float32)
    scale = 1.0 / (LOOK_RNG * LOOK_AZ)
    for n, (one, two) in enumerate(pairs):
        bit = (one ^ two).bit_length() - 1
        for r in range(rows):
            l = r // LOOK_RNG
            look[:, one, bit, l, n, r] = scale
            look[0, two, bit, l, n, r] = scale
            look[1, two, bit, l, n, r] = -scale
    look = look.reshape(2, acqs * bits * looks, len(pairs) * rows)
    return pairs, twist, fwd, inv, pool, look


def matched_filter(rate, length):
    inner = length // OUTER
    index = (
        jnp.arange(OUTER, dtype=jnp.int32)[:, None]
        + OUTER * jnp.arange(inner, dtype=jnp.int32)[None, :]
    )
    signed = jnp.where(index < length // 2, index, index - length).astype(jnp.float32)
    quad = signed * signed / length
    phase = (jnp.pi * rate)[None, :, None] * quad[:, None, :]
    return jnp.stack([jnp.cos(phase), -jnp.sin(phase)]) / length


def focus_call(x, filt, acqs):
    rows, local = x.shape[2], x.shape[3]
    length = x.shape[0] // acqs * local
    inner = length // OUTER
    pairs, twist, fwd, inv, pool, look = focus_tables(acqs, rows, length)
    return pl.pallas_call(
        functools.partial(focus_kernel, acqs, pairs),
        out_shape=jax.ShapeDtypeStruct((2, look.shape[1], length // LOOK_AZ), jnp.float32),
        in_specs=[pl.BlockSpec(memory_space=pltpu.VMEM)] * 7,
        out_specs=pl.BlockSpec(memory_space=pltpu.VMEM),
        scratch_shapes=[
            pltpu.VMEM((acqs, OUTER, rows, 2 * inner), jnp.bfloat16),
            pltpu.VMEM((acqs, OUTER, rows, 2 * inner), jnp.float32),
            pltpu.VMEM((4 * len(pairs) * rows, pool.shape[0]), jnp.bfloat16),
        ],
        compiler_params=pltpu.CompilerParams(vmem_limit_bytes=48 * 2**20),
        name="focus",
    )(x, filt, jnp.asarray(twist), jnp.asarray(fwd), jnp.asarray(inv), jnp.asarray(pool),
      jnp.asarray(look))


def per_device_joint(raw_echo, chirp_phase, pulse_counts, azimuth_rate, partner_bits):
    echoes = raw_echo[0].transpose(2, 0, 1)
    pulses_dev = echoes.shape[2]
    acqs, turns = lax.axis_size("acq"), lax.axis_size("pulse")
    bits = acqs.bit_length() - 1
    rows = RNG // (acqs * turns)
    looks = rows // LOOK_RNG
    first = lax.axis_index("pulse") * pulses_dev
    counts = jnp.stack([pulse_counts[0], first.astype(jnp.int32)])
    x = compress_call(echoes, jnp.repeat(chirp_phase, 2)[None], counts, acqs * turns)
    rate = lax.dynamic_slice(azimuth_rate, (lax.axis_index("acq") * rows,), (rows,))
    filt = matched_filter(rate, pulses_dev * turns)
    out = focus_call(x, filt, acqs)
    cells = out.shape[2]
    out = out.reshape(2, acqs, bits * looks, cells)
    out = lax.all_to_all(out, "acq", split_axis=1, concat_axis=1, tiled=True)
    out = out.reshape(2, acqs, bits, looks, cells).transpose(0, 2, 1, 3, 4)
    out = out.reshape(2, bits, acqs * looks, cells)
    chosen = partner_bits[0]
    slots = []
    for slot in range(2):
        taken = out[:, 0]
        for which in range(1, bits):
            taken = jnp.where(chosen[slot] == which, out[:, which], taken)
        slots.append(taken)
    return (
        jnp.stack([item[0] for item in slots])[None],
        jnp.stack([item[1] for item in slots])[None],
    )


def solution(mesh):
    in_specs = (P("acq", None, "pulse", None), P(), P("acq"), P("pulse"), P("acq", None))
    out_specs = (P("acq", None, "pulse", None), P("acq", None, "pulse", None))
    devices = mesh.shape["acq"] * mesh.shape["pulse"]
    joint = RNG % (16 * devices) == 0
    return jax.shard_map(
        per_device_joint if joint else per_device,
        mesh=mesh, in_specs=in_specs, out_specs=out_specs, check_vma=False,
    )
```

```python
import functools
import math

import jax
import jax.numpy as jnp
import numpy as np
from jax import lax
from jax.experimental import pallas as pl
from jax.experimental.pallas import tpu as pltpu
from jax.sharding import PartitionSpec as P

RNG = 512
TAPS = 1024
LOOK_RNG = 4
LOOK_AZ = 16


def partner_2(shard, axis, bit):
    return lax.ppermute(shard, axis, [(i, i ^ 1 << bit) for i in range(lax.axis_size(axis))])


def part_tables(length, inverse):
    steps = jnp.arange(length, dtype=jnp.int32)
    angle = 2.0 * jnp.pi * (steps[:, None] * steps[None, :] % length).astype(jnp.float32) / length
    cosine = jnp.cos(angle)
    sine = jnp.sin(angle)
    if inverse:
        sine = -sine
    return jnp.stack([jnp.stack([cosine, -sine]), jnp.stack([sine, cosine])])


def complex_product(left_re, left_im, right_re, right_im):
    return (left_re * right_re - left_im * right_im, left_re * right_im + left_im * right_re)


def compress(echoes, toeplitz, first_pulse, live_pulses, block_cols, window):
    pulse_rows = echoes.shape[1]
    parts_re = []
    parts_im = []
    for start in range(0, RNG, block_cols):
        segment = echoes[:, :, start : start + window]
        stacked = jnp.concatenate([segment[0], segment[1]], axis=1)
        result = lax.dot_general(
            toeplitz, stacked, (((1,), (1,)), ((), ())), preferred_element_type=jnp.float32
        )
        parts_re.append(result[:block_cols])
        parts_im.append(result[block_cols:])
    joined = jnp.stack([jnp.concatenate(parts_re, axis=0), jnp.concatenate(parts_im, axis=0)])
    pulse_ids = first_pulse + jnp.arange(pulse_rows, dtype=jnp.int32)
    keep = (pulse_ids < live_pulses).astype(jnp.float32)
    return (joined * keep[None, None, :]).astype(jnp.bfloat16)


def azimuth(turned, azimuth_rate):
    columns = turned.shape[1]
    length = turned.shape[2]
    outer_len = 64
    inner_len = length // outer_len
    highest = lax.Precision.HIGHEST
    signal = turned.astype(jnp.float32).reshape(2, columns, outer_len, inner_len)
    section_one = jnp.einsum(
        "pcab,pqak->qckb", signal, part_tables(outer_len, False), precision=highest
    )
    outer_ids = jnp.arange(outer_len, dtype=jnp.int32)
    inner_ids = jnp.arange(inner_len, dtype=jnp.int32)
    twist = (
        2.0
        * jnp.pi
        * (outer_ids[:, None] * inner_ids[None, :] % length).astype(jnp.float32)
        / length
    )
    twist_cos = jnp.cos(twist)
    twist_sin = jnp.sin(twist)
    turned_re, turned_im = complex_product(section_one[0], section_one[1], twist_cos, -twist_sin)
    spectrum = jnp.einsum(
        "pckb,pqbm->qckm",
        jnp.stack([turned_re, turned_im]),
        part_tables(inner_len, False),
        precision=highest,
    )
    freq_index = outer_ids[:, None] + outer_len * inner_ids[None, :]
    signed = jnp.where(freq_index < length // 2, freq_index, freq_index - length).astype(
        jnp.float32
    )
    quad = signed * signed / length
    phase = (jnp.pi * azimuth_rate)[:, None, None] * quad[None, :, :]
    filt_re, filt_im = complex_product(spectrum[0], spectrum[1], jnp.cos(phase), -jnp.sin(phase))
    back_one = jnp.einsum(
        "pckm,pqmb->qckb",
        jnp.stack([filt_re, filt_im]),
        part_tables(inner_len, True),
        precision=highest,
    )
    undo_re, undo_im = complex_product(back_one[0], back_one[1], twist_cos, twist_sin)
    restored = jnp.einsum(
        "pckb,pqka->qcab",
        jnp.stack([undo_re, undo_im]),
        part_tables(outer_len, True),
        precision=highest,
    )
    return (restored / length).reshape(2, columns, length)


def multilook(values):
    columns = values.shape[0]
    pulse_len = values.shape[1]
    shaped = values.reshape(columns // LOOK_RNG, LOOK_RNG, pulse_len // LOOK_AZ, LOOK_AZ)
    return jnp.mean(shaped, axis=(1, 3))


def cross_looks(own_block, partner):
    own_f = own_block.astype(jnp.float32)
    other_f = partner.astype(jnp.float32)
    prod_re = own_f[0] * other_f[0] + own_f[1] * other_f[1]
    prod_im = own_f[1] * other_f[0] - own_f[0] * other_f[1]
    return jnp.stack([multilook(prod_re), multilook(prod_im)])


def per_device(raw_echo, chirp_phase, pulse_counts, azimuth_rate, partner_bits):
    echoes = raw_echo[0]
    pulses_dev = echoes.shape[1]
    block_cols = min(256, RNG)
    window = block_cols + TAPS - 1
    amplitude = 2.0 / math.sqrt(TAPS)
    table_re = (amplitude * jnp.cos(chirp_phase)).astype(jnp.bfloat16)
    table_im = (amplitude * jnp.sin(chirp_phase)).astype(jnp.bfloat16)
    padding = jnp.zeros((block_cols,), jnp.bfloat16)
    band_re = jnp.tile(jnp.concatenate([table_re, padding]), block_cols)[
        : block_cols * window
    ].reshape(block_cols, window)
    band_im = jnp.tile(jnp.concatenate([table_im, padding]), block_cols)[
        : block_cols * window
    ].reshape(block_cols, window)
    toeplitz = jnp.concatenate(
        [jnp.concatenate([band_re, band_im], axis=1), jnp.concatenate([-band_im, band_re], axis=1)],
        axis=0,
    )
    live_pulses = pulse_counts[0]
    first_pulse = lax.axis_index("pulse") * pulses_dev
    compressed = compress(echoes, toeplitz, first_pulse, live_pulses, block_cols, window)
    turned = lax.all_to_all(compressed, "pulse", split_axis=1, concat_axis=2, tiled=True)
    focused = azimuth(turned, azimuth_rate).astype(jnp.bfloat16)
    chosen = partner_bits[0]
    bit_count = lax.axis_size("acq").bit_length() - 1
    arrived = [partner_2(focused, "acq", which) for which in range(bit_count)]
    results = []
    for slot in range(2):
        partner = arrived[0]
        for which in range(1, bit_count):
            partner = jnp.where(chosen[slot] == which, arrived[which], partner)
        results.append(cross_looks(focused, partner))
    interfere_real = jnp.stack([item[0] for item in results])[None]
    interfere_imag = jnp.stack([item[1] for item in results])[None]
    return (interfere_real, interfere_imag)


OUTER = 16


def butterflies(values, sign):
    count = len(values)
    if count == 1:
        return values
    even = butterflies(values[0::2], sign)
    odd = butterflies(values[1::2], sign)
    low, high = [], []
    for k in range(count // 2):
        e_re, e_im = even[k]
        o_re, o_im = odd[k]
        if k == 0:
            t_re, t_im = o_re, o_im
        elif 4 * k == count:
            t_re, t_im = (-o_im, o_re) if sign > 0 else (o_im, -o_re)
        else:
            c = math.cos(2.0 * math.pi * k / count)
            s = sign * math.sin(2.0 * math.pi * k / count)
            t_re, t_im = o_re * c - o_im * s, o_re * s + o_im * c
        low.append((e_re + t_re, e_im + t_im))
        high.append((e_re - t_re, e_im - t_im))
    return low + high


def compress_kernel(
    block_cols, counts_ref, phase_ref, rate_ref, echo_ref, turned_ref, filt_ref, band, ready, send_sem, recv_sem,
    own_sem,
):
    step = pl.program_id(0)
    steps = pl.num_programs(0)
    acqs = lax.axis_size("acq")
    devices = acqs * lax.axis_size("pulse")
    me = lax.axis_index("pulse") * acqs + lax.axis_index("acq")
    barrier = pltpu.get_barrier_semaphore()

    def place(d):
        peer = me ^ d
        return peer, (peer % acqs, peer // acqs)

    @pl.when(step == 0)
    def _():
        def greet(d, carry):
            pl.semaphore_signal(
                barrier, inc=1, device_id=place(d)[1], device_id_type=pl.DeviceIdType.MESH
            )
            return carry

        lax.fori_loop(1, devices, greet, 0)

    pulses = echo_ref.shape[2]
    width = band.shape[2]
    window = block_cols + TAPS - 1

    @pl.when(step == 0)
    def _():
        amplitude = 2.0 / math.sqrt(TAPS)
        phase = phase_ref[...]
        cosine, sine = amplitude * jnp.cos(phase), amplitude * jnp.sin(phase)
        even = lax.broadcasted_iota(jnp.int32, phase.shape, 1) % 2 == 0
        for part, table in enumerate(
            (jnp.where(even, cosine, sine), jnp.where(even, -sine, cosine))
        ):
            row = jnp.concatenate(
                [table, jnp.zeros((1, width - 2 * TAPS), jnp.float32)], axis=1
            )
            rows = jnp.broadcast_to(row, (block_cols, width))
            band[part] = pltpu.roll(rows, 0, 1, stride=2, stride_axis=0).astype(jnp.bfloat16)

    first = counts_ref[1] + step * pulses
    ids = first + lax.broadcasted_iota(jnp.int32, (1, pulses), 1)
    keep = ids < counts_ref[0]
    per = ready.shape[3]
    slabs = block_cols // per
    for block in range(RNG // block_cols):
        echo = echo_ref[pl.ds(block * block_cols, window)].reshape(2 * window, pulses)
        for part in range(2):
            y = jnp.dot(
                band[part, :, : 2 * window], echo, preferred_element_type=jnp.float32
            )
            kept = jnp.where(keep, y, 0.0).astype(jnp.bfloat16)
            ready[step, pl.ds(block * slabs, slabs), part] = kept.reshape(slabs, per, pulses)

    @pl.when(step == 0)
    def _():
        pl.semaphore_wait(barrier, devices - 1)

    def remote(at, d):
        peer, where = place(d)
        lanes = pl.ds(pl.multiple_of(at * pulses, 128), pulses)
        return pltpu.make_async_remote_copy(
            src_ref=ready.at[at, peer],
            dst_ref=turned_ref.at[me, :, :, lanes],
            send_sem=send_sem.at[at, d],
            recv_sem=recv_sem.at[at, d],
            device_id=where,
            device_id_type=pl.DeviceIdType.MESH,
        )

    def own(at):
        lanes = pl.ds(pl.multiple_of(at * pulses, 128), pulses)
        return pltpu.make_async_copy(
            ready.at[at, me], turned_ref.at[me, :, :, lanes], own_sem.at[at]
        )

    half = devices // 2

    def send(i, carry):
        remote(step, devices - 1 - i).start()
        remote(step, half - 1 - i).start()
        return carry

    lax.fori_loop(0, half - 1, send, 0)
    remote(step, half).start()
    own(step).start()

    @pl.when(step == steps - 1)
    def _():
        outer, rows, inner = filt_ref.shape[1:]
        length = outer * inner
        rate = jnp.pi * rate_ref[...]

        def matched(k, carry):
            index = k + outer * lax.broadcasted_iota(jnp.int32, (1, inner), 1)
            signed = jnp.where(index < length // 2, index, index - length).astype(jnp.float32)
            phase = rate * (signed * signed / length)
            filt_ref[0, k] = jnp.cos(phase) / length
            filt_ref[1, k] = -jnp.sin(phase) / length
            return carry

        lax.fori_loop(0, outer, matched, 0)

        def finish(i, carry):
            remote(i // (devices - 1), i % (devices - 1) + 1).wait()
            return carry

        lax.fori_loop(0, steps * (devices - 1), finish, 0)
        for at in range(ready.shape[0]):
            own(at).wait()


def compress_call(echoes, phase, rate, counts, devices, length):
    pulses = echoes.shape[2]
    step = min(256, pulses)
    steps = pulses // step
    block_cols = 256
    width = -(-2 * (block_cols + TAPS - 1) // 128) * 128
    per = RNG // devices
    return pl.pallas_call(
        functools.partial(compress_kernel, block_cols),
        grid=(steps,),
        out_shape=(
            jax.ShapeDtypeStruct((devices, 2, per, pulses), jnp.bfloat16),
            jax.ShapeDtypeStruct((2, OUTER, per, length // OUTER), jnp.float32),
        ),
        in_specs=[
            pl.BlockSpec(memory_space=pltpu.SMEM),
            pl.BlockSpec((1, 2 * TAPS), lambda i: (0, 0)),
            pl.BlockSpec((per, 1), lambda i: (0, 0)),
            pl.BlockSpec((echoes.shape[0], 2, step), lambda i: (0, 0, i)),
        ],
        out_specs=(
            pl.BlockSpec(memory_space=pl.ANY),
            pl.BlockSpec((2, OUTER, per, length // OUTER), lambda i: (0, 0, 0, 0)),
        ),
        scratch_shapes=[
            pltpu.VMEM((2, block_cols, width), jnp.bfloat16),
            pltpu.VMEM((steps, devices, 2, per, step), jnp.bfloat16),
            pltpu.SemaphoreType.DMA((steps, devices)),
            pltpu.SemaphoreType.DMA((steps, devices)),
            pltpu.SemaphoreType.DMA((steps,)),
        ],
        compiler_params=pltpu.CompilerParams(
            vmem_limit_bytes=40 * 2**20, collective_id=0, has_side_effects=True
        ),
        name="compress",
    )(counts, phase, rate, echoes)


def focus_kernel(
    acqs, pairs, x_ref, filt_ref, twist_ref, fwd_ref, inv_ref, pool_ref, look_ref, out_ref,
    held, image, prods,
):
    rows = x_ref.shape[2]
    local = x_ref.shape[3]
    inner = twist_ref.shape[2]
    per_src = local // inner
    chunk = 128

    def forward(index, carry):
        acq, at = index // (inner // chunk), index % (inner // chunk)
        values = []
        for a in range(OUTER):
            src = (a // per_src) * acqs + acq
            lane = pl.multiple_of((a % per_src) * inner + at * chunk, chunk)
            values.append(
                tuple(
                    x_ref[src, part, :, pl.ds(lane, chunk)].astype(jnp.float32)
                    for part in range(2)
                )
            )
        lane = pl.multiple_of(at * chunk, chunk)
        for k, (re, im) in enumerate(butterflies(values, -1)):
            c = twist_ref[0, pl.ds(k, 1), pl.ds(lane, chunk)]
            s = twist_ref[1, pl.ds(k, 1), pl.ds(lane, chunk)]
            held[acq, k, :, pl.ds(lane, chunk)] = (re * c + im * s).astype(jnp.bfloat16)
            lane_im = pl.multiple_of(lane + inner, chunk)
            held[acq, k, :, pl.ds(lane_im, chunk)] = (im * c - re * s).astype(jnp.bfloat16)
        return carry

    def middle(acq, carry):
        spec = jnp.dot(
            held[acq].reshape(OUTER * rows, 2 * inner),
            fwd_ref[...],
            preferred_element_type=jnp.float32,
        )
        s_re, s_im = spec[:, :inner], spec[:, inner:]
        f_re = filt_ref[0].reshape(OUTER * rows, inner)
        f_im = filt_ref[1].reshape(OUTER * rows, inner)
        m_re = (s_re * f_re - s_im * f_im).astype(jnp.bfloat16)
        m_im = (s_re * f_im + s_im * f_re).astype(jnp.bfloat16)
        back = jnp.dot(
            jnp.concatenate([m_re, m_im], axis=1), inv_ref[...],
            preferred_element_type=jnp.float32,
        )
        image[acq] = back.reshape(OUTER, rows, 2 * inner)
        return carry

    def inverse(index, carry):
        acq, at = index // (inner // chunk), index % (inner // chunk)
        lane = pl.multiple_of(at * chunk, chunk)
        lane_im = pl.multiple_of(lane + inner, chunk)
        values = []
        for k in range(OUTER):
            re = image[acq, k, :, pl.ds(lane, chunk)]
            im = image[acq, k, :, pl.ds(lane_im, chunk)]
            c = twist_ref[0, pl.ds(k, 1), pl.ds(lane, chunk)]
            s = twist_ref[1, pl.ds(k, 1), pl.ds(lane, chunk)]
            values.append((re * c - im * s, im * c + re * s))
        for a, (re, im) in enumerate(butterflies(values, 1)):
            image[acq, a, :, pl.ds(lane, chunk)] = re
            image[acq, a, :, pl.ds(lane_im, chunk)] = im
        return carry

    lax.fori_loop(0, acqs * (inner // chunk), forward, 0)
    lax.fori_loop(0, acqs, middle, 0)
    lax.fori_loop(0, acqs * (inner // chunk), inverse, 0)

    group = pool_ref.shape[0] // inner
    count = len(pairs) * rows
    parts = [[], []]
    for g in range(OUTER // group):
        for step in range(group):
            a = g * group + step
            lanes = pl.ds(step * inner, inner)
            for n, (one, two) in enumerate(pairs):
                o_re, o_im = image[one, a, :, :inner], image[one, a, :, inner:]
                t_re, t_im = image[two, a, :, :inner], image[two, a, :, inner:]
                for part, p in enumerate(
                    (o_re * t_re + o_im * t_im, o_im * t_re - o_re * t_im)
                ):
                    top = p.astype(jnp.bfloat16)
                    rest = (p - top.astype(jnp.float32)).astype(jnp.bfloat16)
                    at = part * count + n * rows
                    prods[pl.ds(at, rows), lanes] = top
                    prods[pl.ds(2 * count + at, rows), lanes] = rest
        z = jnp.dot(prods[...], pool_ref[...], preferred_element_type=jnp.float32)
        z = z[: 2 * count] + z[2 * count :]
        parts[0].append(z[:count])
        parts[1].append(z[count:])
    for part in range(2):
        out_ref[part] = jnp.dot(
            look_ref[part], jnp.concatenate(parts[part], axis=1),
            preferred_element_type=jnp.float32, precision=lax.Precision.HIGHEST,
        )


def focus_tables(acqs, rows, length):
    inner = length // OUTER
    b = np.arange(inner)
    angle = 2.0 * np.pi * (b[:, None] * b[None, :] % inner) / inner
    c, s = np.cos(angle), np.sin(angle)
    fwd = np.block([[c, -s], [s, c]]).astype(jnp.bfloat16)
    inv = np.block([[c, s], [-s, c]]).astype(jnp.bfloat16)
    angle = 2.0 * np.pi * (np.arange(OUTER)[:, None] * b[None, :]) / length
    twist = np.stack([np.cos(angle), np.sin(angle)]).astype(np.float32)
    span = 128 * LOOK_AZ
    pool = (np.arange(span)[:, None] // LOOK_AZ == np.arange(128)[None, :]).astype(jnp.bfloat16)
    bits = acqs.bit_length() - 1
    pairs = [(a, a ^ 1 << bit) for bit in range(bits) for a in range(acqs) if not a >> bit & 1]
    looks = rows // LOOK_RNG
    look = np.zeros((2, acqs, bits, looks, len(pairs), rows), np.float32)
    scale = 1.0 / (LOOK_RNG * LOOK_AZ)
    for n, (one, two) in enumerate(pairs):
        bit = (one ^ two).bit_length() - 1
        for r in range(rows):
            l = r // LOOK_RNG
            look[:, one, bit, l, n, r] = scale
            look[0, two, bit, l, n, r] = scale
            look[1, two, bit, l, n, r] = -scale
    look = look.reshape(2, acqs * bits * looks, len(pairs) * rows)
    return pairs, twist, fwd, inv, pool, look


def focus_call(x, filt, acqs):
    rows, local = x.shape[2], x.shape[3]
    length = x.shape[0] // acqs * local
    inner = length // OUTER
    pairs, twist, fwd, inv, pool, look = focus_tables(acqs, rows, length)
    return pl.pallas_call(
        functools.partial(focus_kernel, acqs, pairs),
        out_shape=jax.ShapeDtypeStruct((2, look.shape[1], length // LOOK_AZ), jnp.float32),
        in_specs=[pl.BlockSpec(memory_space=pltpu.VMEM)] * 7,
        out_specs=pl.BlockSpec(memory_space=pltpu.VMEM),
        scratch_shapes=[
            pltpu.VMEM((acqs, OUTER, rows, 2 * inner), jnp.bfloat16),
            pltpu.VMEM((acqs, OUTER, rows, 2 * inner), jnp.float32),
            pltpu.VMEM((4 * len(pairs) * rows, pool.shape[0]), jnp.bfloat16),
        ],
        compiler_params=pltpu.CompilerParams(vmem_limit_bytes=48 * 2**20),
        name="focus",
    )(x, filt, jnp.asarray(twist), jnp.asarray(fwd), jnp.asarray(inv), jnp.asarray(pool),
      jnp.asarray(look))


def per_device_joint(raw_echo, chirp_phase, pulse_counts, azimuth_rate, partner_bits):
    echoes = raw_echo[0].transpose(2, 0, 1)
    pulses_dev = echoes.shape[2]
    acqs, turns = lax.axis_size("acq"), lax.axis_size("pulse")
    bits = acqs.bit_length() - 1
    rows = RNG // (acqs * turns)
    looks = rows // LOOK_RNG
    first = lax.axis_index("pulse") * pulses_dev
    counts = jnp.stack([pulse_counts[0], first.astype(jnp.int32)])
    rate = lax.dynamic_slice(azimuth_rate, (lax.axis_index("acq") * rows,), (rows,))
    x, filt = compress_call(
        echoes, jnp.repeat(chirp_phase, 2)[None], rate[:, None], counts, acqs * turns,
        pulses_dev * turns,
    )
    out = focus_call(x, filt, acqs)
    cells = out.shape[2]
    out = out.reshape(2, acqs, bits * looks, cells)
    out = lax.all_to_all(out, "acq", split_axis=1, concat_axis=1, tiled=True)
    out = out.reshape(2, acqs, bits, looks, cells).transpose(0, 2, 1, 3, 4)
    out = out.reshape(2, bits, acqs * looks, cells)
    chosen = partner_bits[0]
    slots = []
    for slot in range(2):
        taken = out[:, 0]
        for which in range(1, bits):
            taken = jnp.where(chosen[slot] == which, out[:, which], taken)
        slots.append(taken)
    return (
        jnp.stack([item[0] for item in slots])[None],
        jnp.stack([item[1] for item in slots])[None],
    )


def solution(mesh):
    in_specs = (P("acq", None, "pulse", None), P(), P("acq"), P("pulse"), P("acq", None))
    out_specs = (P("acq", None, "pulse", None), P("acq", None, "pulse", None))
    devices = mesh.shape["acq"] * mesh.shape["pulse"]
    joint = RNG % (16 * devices) == 0
    return jax.shard_map(
        per_device_joint if joint else per_device,
        mesh=mesh, in_specs=in_specs, out_specs=out_specs, check_vma=False,
    )
```

```python
import functools
import math

import jax
import jax.numpy as jnp
import numpy as np
from jax import lax
from jax.experimental import pallas as pl
from jax.experimental.pallas import tpu as pltpu
from jax.sharding import PartitionSpec as P

RNG = 512
TAPS = 1024
LOOK_RNG = 4
LOOK_AZ = 16


def partner_2(shard, axis, bit):
    return lax.ppermute(shard, axis, [(i, i ^ 1 << bit) for i in range(lax.axis_size(axis))])


def part_tables(length, inverse):
    steps = jnp.arange(length, dtype=jnp.int32)
    angle = 2.0 * jnp.pi * (steps[:, None] * steps[None, :] % length).astype(jnp.float32) / length
    cosine = jnp.cos(angle)
    sine = jnp.sin(angle)
    if inverse:
        sine = -sine
    return jnp.stack([jnp.stack([cosine, -sine]), jnp.stack([sine, cosine])])


def complex_product(left_re, left_im, right_re, right_im):
    return (left_re * right_re - left_im * right_im, left_re * right_im + left_im * right_re)


def compress(echoes, toeplitz, first_pulse, live_pulses, block_cols, window):
    pulse_rows = echoes.shape[1]
    parts_re = []
    parts_im = []
    for start in range(0, RNG, block_cols):
        segment = echoes[:, :, start : start + window]
        stacked = jnp.concatenate([segment[0], segment[1]], axis=1)
        result = lax.dot_general(
            toeplitz, stacked, (((1,), (1,)), ((), ())), preferred_element_type=jnp.float32
        )
        parts_re.append(result[:block_cols])
        parts_im.append(result[block_cols:])
    joined = jnp.stack([jnp.concatenate(parts_re, axis=0), jnp.concatenate(parts_im, axis=0)])
    pulse_ids = first_pulse + jnp.arange(pulse_rows, dtype=jnp.int32)
    keep = (pulse_ids < live_pulses).astype(jnp.float32)
    return (joined * keep[None, None, :]).astype(jnp.bfloat16)


def azimuth(turned, azimuth_rate):
    columns = turned.shape[1]
    length = turned.shape[2]
    outer_len = 64
    inner_len = length // outer_len
    highest = lax.Precision.HIGHEST
    signal = turned.astype(jnp.float32).reshape(2, columns, outer_len, inner_len)
    section_one = jnp.einsum(
        "pcab,pqak->qckb", signal, part_tables(outer_len, False), precision=highest
    )
    outer_ids = jnp.arange(outer_len, dtype=jnp.int32)
    inner_ids = jnp.arange(inner_len, dtype=jnp.int32)
    twist = (
        2.0
        * jnp.pi
        * (outer_ids[:, None] * inner_ids[None, :] % length).astype(jnp.float32)
        / length
    )
    twist_cos = jnp.cos(twist)
    twist_sin = jnp.sin(twist)
    turned_re, turned_im = complex_product(section_one[0], section_one[1], twist_cos, -twist_sin)
    spectrum = jnp.einsum(
        "pckb,pqbm->qckm",
        jnp.stack([turned_re, turned_im]),
        part_tables(inner_len, False),
        precision=highest,
    )
    freq_index = outer_ids[:, None] + outer_len * inner_ids[None, :]
    signed = jnp.where(freq_index < length // 2, freq_index, freq_index - length).astype(
        jnp.float32
    )
    quad = signed * signed / length
    phase = (jnp.pi * azimuth_rate)[:, None, None] * quad[None, :, :]
    filt_re, filt_im = complex_product(spectrum[0], spectrum[1], jnp.cos(phase), -jnp.sin(phase))
    back_one = jnp.einsum(
        "pckm,pqmb->qckb",
        jnp.stack([filt_re, filt_im]),
        part_tables(inner_len, True),
        precision=highest,
    )
    undo_re, undo_im = complex_product(back_one[0], back_one[1], twist_cos, twist_sin)
    restored = jnp.einsum(
        "pckb,pqka->qcab",
        jnp.stack([undo_re, undo_im]),
        part_tables(outer_len, True),
        precision=highest,
    )
    return (restored / length).reshape(2, columns, length)


def multilook(values):
    columns = values.shape[0]
    pulse_len = values.shape[1]
    shaped = values.reshape(columns // LOOK_RNG, LOOK_RNG, pulse_len // LOOK_AZ, LOOK_AZ)
    return jnp.mean(shaped, axis=(1, 3))


def cross_looks(own_block, partner):
    own_f = own_block.astype(jnp.float32)
    other_f = partner.astype(jnp.float32)
    prod_re = own_f[0] * other_f[0] + own_f[1] * other_f[1]
    prod_im = own_f[1] * other_f[0] - own_f[0] * other_f[1]
    return jnp.stack([multilook(prod_re), multilook(prod_im)])


def per_device(raw_echo, chirp_phase, pulse_counts, azimuth_rate, partner_bits):
    echoes = raw_echo[0]
    pulses_dev = echoes.shape[1]
    block_cols = min(256, RNG)
    window = block_cols + TAPS - 1
    amplitude = 2.0 / math.sqrt(TAPS)
    table_re = (amplitude * jnp.cos(chirp_phase)).astype(jnp.bfloat16)
    table_im = (amplitude * jnp.sin(chirp_phase)).astype(jnp.bfloat16)
    padding = jnp.zeros((block_cols,), jnp.bfloat16)
    band_re = jnp.tile(jnp.concatenate([table_re, padding]), block_cols)[
        : block_cols * window
    ].reshape(block_cols, window)
    band_im = jnp.tile(jnp.concatenate([table_im, padding]), block_cols)[
        : block_cols * window
    ].reshape(block_cols, window)
    toeplitz = jnp.concatenate(
        [jnp.concatenate([band_re, band_im], axis=1), jnp.concatenate([-band_im, band_re], axis=1)],
        axis=0,
    )
    live_pulses = pulse_counts[0]
    first_pulse = lax.axis_index("pulse") * pulses_dev
    compressed = compress(echoes, toeplitz, first_pulse, live_pulses, block_cols, window)
    turned = lax.all_to_all(compressed, "pulse", split_axis=1, concat_axis=2, tiled=True)
    focused = azimuth(turned, azimuth_rate).astype(jnp.bfloat16)
    chosen = partner_bits[0]
    bit_count = lax.axis_size("acq").bit_length() - 1
    arrived = [partner_2(focused, "acq", which) for which in range(bit_count)]
    results = []
    for slot in range(2):
        partner = arrived[0]
        for which in range(1, bit_count):
            partner = jnp.where(chosen[slot] == which, arrived[which], partner)
        results.append(cross_looks(focused, partner))
    interfere_real = jnp.stack([item[0] for item in results])[None]
    interfere_imag = jnp.stack([item[1] for item in results])[None]
    return (interfere_real, interfere_imag)


OUTER = 16


def butterflies(values, sign):
    count = len(values)
    if count == 1:
        return values
    even = butterflies(values[0::2], sign)
    odd = butterflies(values[1::2], sign)
    low, high = [], []
    for k in range(count // 2):
        e_re, e_im = even[k]
        o_re, o_im = odd[k]
        if k == 0:
            t_re, t_im = o_re, o_im
        elif 4 * k == count:
            t_re, t_im = (-o_im, o_re) if sign > 0 else (o_im, -o_re)
        else:
            c = math.cos(2.0 * math.pi * k / count)
            s = sign * math.sin(2.0 * math.pi * k / count)
            t_re, t_im = o_re * c - o_im * s, o_re * s + o_im * c
        low.append((e_re + t_re, e_im + t_im))
        high.append((e_re - t_re, e_im - t_im))
    return low + high


def compress_kernel(
    block_cols, counts_ref, phase_ref, rate_ref, echo_ref, turned_ref, filt_ref, band, ready, send_sem, recv_sem,
    own_sem,
):
    step = pl.program_id(0)
    steps = pl.num_programs(0)
    acqs = lax.axis_size("acq")
    devices = acqs * lax.axis_size("pulse")
    me = lax.axis_index("pulse") * acqs + lax.axis_index("acq")
    barrier = pltpu.get_barrier_semaphore()

    def place(d):
        peer = me ^ d
        return peer, (peer % acqs, peer // acqs)

    @pl.when(step == 0)
    def _():
        def greet(d, carry):
            pl.semaphore_signal(
                barrier, inc=1, device_id=place(d)[1], device_id_type=pl.DeviceIdType.MESH
            )
            return carry

        lax.fori_loop(1, devices, greet, 0)

    pulses = echo_ref.shape[2]
    width = band.shape[2]
    window = block_cols + TAPS - 1

    @pl.when(step == 0)
    def _():
        amplitude = 2.0 / math.sqrt(TAPS)
        phase = phase_ref[...]
        cosine, sine = amplitude * jnp.cos(phase), amplitude * jnp.sin(phase)
        even = lax.broadcasted_iota(jnp.int32, phase.shape, 1) % 2 == 0
        for part, table in enumerate(
            (jnp.where(even, cosine, sine), jnp.where(even, -sine, cosine))
        ):
            row = jnp.concatenate(
                [table, jnp.zeros((1, width - 2 * TAPS), jnp.float32)], axis=1
            )
            rows = jnp.broadcast_to(row, (block_cols, width))
            band[part] = pltpu.roll(rows, 0, 1, stride=2, stride_axis=0).astype(jnp.bfloat16)

    first = counts_ref[1] + step * pulses
    ids = first + lax.broadcasted_iota(jnp.int32, (1, pulses), 1)
    keep = ids < counts_ref[0]
    per = ready.shape[3]
    slabs = block_cols // per
    for block in range(RNG // block_cols):
        echo = echo_ref[pl.ds(block * block_cols, window)].reshape(2 * window, pulses)
        for part in range(2):
            y = jnp.dot(
                band[part, :, : 2 * window], echo, preferred_element_type=jnp.float32
            )
            kept = jnp.where(keep, y, 0.0).astype(jnp.bfloat16)
            ready[step, pl.ds(block * slabs, slabs), part] = kept.reshape(slabs, per, pulses)

    @pl.when(step == 0)
    def _():
        pl.semaphore_wait(barrier, devices - 1)

    def remote(at, d):
        peer, where = place(d)
        lanes = pl.ds(pl.multiple_of(at * pulses, 128), pulses)
        return pltpu.make_async_remote_copy(
            src_ref=ready.at[at, peer],
            dst_ref=turned_ref.at[me, :, :, lanes],
            send_sem=send_sem.at[at, d],
            recv_sem=recv_sem.at[at, d],
            device_id=where,
            device_id_type=pl.DeviceIdType.MESH,
        )

    def own(at):
        lanes = pl.ds(pl.multiple_of(at * pulses, 128), pulses)
        return pltpu.make_async_copy(
            ready.at[at, me], turned_ref.at[me, :, :, lanes], own_sem.at[at]
        )

    half = devices // 2

    def send(i, carry):
        remote(step, devices - 1 - i).start()
        remote(step, half - 1 - i).start()
        return carry

    lax.fori_loop(0, half - 1, send, 0)
    remote(step, half).start()
    own(step).start()

    @pl.when(step == steps - 1)
    def _():
        outer, rows, inner = filt_ref.shape[1:]
        length = outer * inner
        rate = jnp.pi * rate_ref[...]

        def matched(k, carry):
            index = k + outer * lax.broadcasted_iota(jnp.int32, (1, inner), 1)
            signed = jnp.where(index < length // 2, index, index - length).astype(jnp.float32)
            phase = rate * (signed * signed / length)
            filt_ref[0, k] = jnp.cos(phase) / length
            filt_ref[1, k] = -jnp.sin(phase) / length
            return carry

        lax.fori_loop(0, outer, matched, 0)

        def finish(i, carry):
            remote(i // (devices - 1), i % (devices - 1) + 1).wait()
            return carry

        lax.fori_loop(0, steps * (devices - 1), finish, 0)
        for at in range(ready.shape[0]):
            own(at).wait()


def compress_call(echoes, phase, rate, counts, devices, length):
    pulses = echoes.shape[2]
    step = min(256, pulses)
    steps = pulses // step
    block_cols = 256
    width = -(-2 * (block_cols + TAPS - 1) // 128) * 128
    per = RNG // devices
    return pl.pallas_call(
        functools.partial(compress_kernel, block_cols),
        grid=(steps,),
        out_shape=(
            jax.ShapeDtypeStruct((devices, 2, per, pulses), jnp.bfloat16),
            jax.ShapeDtypeStruct((2, OUTER, per, length // OUTER), jnp.float32),
        ),
        in_specs=[
            pl.BlockSpec(memory_space=pltpu.SMEM),
            pl.BlockSpec((1, 2 * TAPS), lambda i: (0, 0)),
            pl.BlockSpec((per, 1), lambda i: (0, 0)),
            pl.BlockSpec((echoes.shape[0], 2, step), lambda i: (0, 0, i)),
        ],
        out_specs=(
            pl.BlockSpec(memory_space=pl.ANY),
            pl.BlockSpec((2, OUTER, per, length // OUTER), lambda i: (0, 0, 0, 0)),
        ),
        scratch_shapes=[
            pltpu.VMEM((2, block_cols, width), jnp.bfloat16),
            pltpu.VMEM((steps, devices, 2, per, step), jnp.bfloat16),
            pltpu.SemaphoreType.DMA((steps, devices)),
            pltpu.SemaphoreType.DMA((steps, devices)),
            pltpu.SemaphoreType.DMA((steps,)),
        ],
        compiler_params=pltpu.CompilerParams(
            vmem_limit_bytes=40 * 2**20, collective_id=0, has_side_effects=True
        ),
        name="compress",
    )(counts, phase, rate, echoes)


def focus_kernel(
    acqs, pairs, chosen_ref, x_ref, filt_ref, twist_ref, fwd_ref, inv_ref, pool_ref, look_ref,
    real_ref, imag_ref, held, image, prods, stage, landed, send_sem, recv_sem, own_sem,
):
    me = lax.axis_index("acq")
    pulse = lax.axis_index("pulse")
    barrier = pltpu.get_barrier_semaphore()
    for d in range(1, acqs):
        pl.semaphore_signal(
            barrier, inc=1, device_id=(me ^ d, pulse), device_id_type=pl.DeviceIdType.MESH
        )
    rows = x_ref.shape[2]
    local = x_ref.shape[3]
    inner = twist_ref.shape[2]
    per_src = local // inner
    chunk = 128

    def forward(index, carry):
        acq, at = index // (inner // chunk), index % (inner // chunk)
        values = []
        for a in range(OUTER):
            src = (a // per_src) * acqs + acq
            lane = pl.multiple_of((a % per_src) * inner + at * chunk, chunk)
            values.append(
                tuple(
                    x_ref[src, part, :, pl.ds(lane, chunk)].astype(jnp.float32)
                    for part in range(2)
                )
            )
        lane = pl.multiple_of(at * chunk, chunk)
        for k, (re, im) in enumerate(butterflies(values, -1)):
            c = twist_ref[0, pl.ds(k, 1), pl.ds(lane, chunk)]
            s = twist_ref[1, pl.ds(k, 1), pl.ds(lane, chunk)]
            held[acq, k, :, pl.ds(lane, chunk)] = (re * c + im * s).astype(jnp.bfloat16)
            lane_im = pl.multiple_of(lane + inner, chunk)
            held[acq, k, :, pl.ds(lane_im, chunk)] = (im * c - re * s).astype(jnp.bfloat16)
        return carry

    def middle(acq, carry):
        spec = jnp.dot(
            held[acq].reshape(OUTER * rows, 2 * inner),
            fwd_ref[...],
            preferred_element_type=jnp.float32,
        )
        s_re, s_im = spec[:, :inner], spec[:, inner:]
        f_re = filt_ref[0].reshape(OUTER * rows, inner)
        f_im = filt_ref[1].reshape(OUTER * rows, inner)
        m_re = (s_re * f_re - s_im * f_im).astype(jnp.bfloat16)
        m_im = (s_re * f_im + s_im * f_re).astype(jnp.bfloat16)
        back = jnp.dot(
            jnp.concatenate([m_re, m_im], axis=1), inv_ref[...],
            preferred_element_type=jnp.float32,
        )
        image[acq] = back.reshape(OUTER, rows, 2 * inner)
        return carry

    def inverse(index, carry):
        acq, at = index // (inner // chunk), index % (inner // chunk)
        lane = pl.multiple_of(at * chunk, chunk)
        lane_im = pl.multiple_of(lane + inner, chunk)
        values = []
        for k in range(OUTER):
            re = image[acq, k, :, pl.ds(lane, chunk)]
            im = image[acq, k, :, pl.ds(lane_im, chunk)]
            c = twist_ref[0, pl.ds(k, 1), pl.ds(lane, chunk)]
            s = twist_ref[1, pl.ds(k, 1), pl.ds(lane, chunk)]
            values.append((re * c - im * s, im * c + re * s))
        for a, (re, im) in enumerate(butterflies(values, 1)):
            image[acq, a, :, pl.ds(lane, chunk)] = re
            image[acq, a, :, pl.ds(lane_im, chunk)] = im
        return carry

    lax.fori_loop(0, acqs * (inner // chunk), forward, 0)
    lax.fori_loop(0, acqs, middle, 0)
    lax.fori_loop(0, acqs * (inner // chunk), inverse, 0)

    group = pool_ref.shape[0] // inner
    count = len(pairs) * rows
    parts = [[], []]
    for g in range(OUTER // group):
        for step in range(group):
            a = g * group + step
            lanes = pl.ds(step * inner, inner)
            for n, (one, two) in enumerate(pairs):
                o_re, o_im = image[one, a, :, :inner], image[one, a, :, inner:]
                t_re, t_im = image[two, a, :, :inner], image[two, a, :, inner:]
                for part, p in enumerate(
                    (o_re * t_re + o_im * t_im, o_im * t_re - o_re * t_im)
                ):
                    top = p.astype(jnp.bfloat16)
                    rest = (p - top.astype(jnp.float32)).astype(jnp.bfloat16)
                    at = part * count + n * rows
                    prods[pl.ds(at, rows), lanes] = top
                    prods[pl.ds(2 * count + at, rows), lanes] = rest
        z = jnp.dot(prods[...], pool_ref[...], preferred_element_type=jnp.float32)
        z = z[: 2 * count] + z[2 * count :]
        parts[0].append(z[:count])
        parts[1].append(z[count:])
    for part in range(2):
        result = jnp.dot(
            look_ref[part], jnp.concatenate(parts[part], axis=1),
            preferred_element_type=jnp.float32, precision=lax.Precision.HIGHEST,
        )
        span = result.shape[0] // acqs
        for acq in range(acqs):
            stage[acq, part] = result[acq * span : (acq + 1) * span]

    pl.semaphore_wait(barrier, acqs - 1)
    copies = [
        pltpu.make_async_remote_copy(
            src_ref=stage.at[me ^ d], dst_ref=landed.at[me],
            send_sem=send_sem.at[d], recv_sem=recv_sem.at[d],
            device_id=(me ^ d, pulse), device_id_type=pl.DeviceIdType.MESH,
        )
        for d in range(1, acqs)
    ]
    copies.append(pltpu.make_async_copy(stage.at[me], landed.at[me], own_sem))
    for copy in copies:
        copy.start()
    for copy in copies:
        copy.wait()
    bits = acqs.bit_length() - 1
    looks = rows // LOOK_RNG
    for part, ref in enumerate((real_ref, imag_ref)):
        for slot in range(2):
            bit = chosen_ref[slot]
            blocks = []
            for src in range(acqs):
                block = landed[src, part]
                taken = block[:looks]
                for which in range(1, bits):
                    taken = jnp.where(
                        bit == which, block[which * looks : (which + 1) * looks], taken
                    )
                blocks.append(taken)
            ref[slot] = jnp.concatenate(blocks, axis=0)


def focus_tables(acqs, rows, length):
    inner = length // OUTER
    b = np.arange(inner)
    angle = 2.0 * np.pi * (b[:, None] * b[None, :] % inner) / inner
    c, s = np.cos(angle), np.sin(angle)
    fwd = np.block([[c, -s], [s, c]]).astype(jnp.bfloat16)
    inv = np.block([[c, s], [-s, c]]).astype(jnp.bfloat16)
    angle = 2.0 * np.pi * (np.arange(OUTER)[:, None] * b[None, :]) / length
    twist = np.stack([np.cos(angle), np.sin(angle)]).astype(np.float32)
    span = 128 * LOOK_AZ
    pool = (np.arange(span)[:, None] // LOOK_AZ == np.arange(128)[None, :]).astype(jnp.bfloat16)
    bits = acqs.bit_length() - 1
    pairs = [(a, a ^ 1 << bit) for bit in range(bits) for a in range(acqs) if not a >> bit & 1]
    looks = rows // LOOK_RNG
    look = np.zeros((2, acqs, bits, looks, len(pairs), rows), np.float32)
    scale = 1.0 / (LOOK_RNG * LOOK_AZ)
    for n, (one, two) in enumerate(pairs):
        bit = (one ^ two).bit_length() - 1
        for r in range(rows):
            l = r // LOOK_RNG
            look[:, one, bit, l, n, r] = scale
            look[0, two, bit, l, n, r] = scale
            look[1, two, bit, l, n, r] = -scale
    look = look.reshape(2, acqs * bits * looks, len(pairs) * rows)
    return pairs, twist, fwd, inv, pool, look


def focus_call(x, filt, chosen, acqs):
    rows, local = x.shape[2], x.shape[3]
    length = x.shape[0] // acqs * local
    inner = length // OUTER
    pairs, twist, fwd, inv, pool, look = focus_tables(acqs, rows, length)
    return pl.pallas_call(
        functools.partial(focus_kernel, acqs, pairs),
        out_shape=(
            jax.ShapeDtypeStruct((2, acqs * rows // LOOK_RNG, length // LOOK_AZ), jnp.float32),
        ) * 2,
        in_specs=[pl.BlockSpec(memory_space=pltpu.SMEM)]
        + [pl.BlockSpec(memory_space=pltpu.VMEM)] * 7,
        out_specs=(pl.BlockSpec(memory_space=pltpu.VMEM),) * 2,
        scratch_shapes=[
            pltpu.VMEM((acqs, OUTER, rows, 2 * inner), jnp.bfloat16),
            pltpu.VMEM((acqs, OUTER, rows, 2 * inner), jnp.float32),
            pltpu.VMEM((4 * len(pairs) * rows, pool.shape[0]), jnp.bfloat16),
            pltpu.VMEM((acqs, 2, look.shape[1] // acqs, length // LOOK_AZ), jnp.float32),
            pltpu.VMEM((acqs, 2, look.shape[1] // acqs, length // LOOK_AZ), jnp.float32),
            pltpu.SemaphoreType.DMA((acqs,)),
            pltpu.SemaphoreType.DMA((acqs,)),
            pltpu.SemaphoreType.DMA,
        ],
        compiler_params=pltpu.CompilerParams(
            vmem_limit_bytes=48 * 2**20, collective_id=1, has_side_effects=True
        ),
        name="focus",
    )(chosen, x, filt, jnp.asarray(twist), jnp.asarray(fwd), jnp.asarray(inv), jnp.asarray(pool),
      jnp.asarray(look))


def per_device_joint(raw_echo, chirp_phase, pulse_counts, azimuth_rate, partner_bits):
    echoes = raw_echo[0].transpose(2, 0, 1)
    pulses_dev = echoes.shape[2]
    acqs, turns = lax.axis_size("acq"), lax.axis_size("pulse")
    rows = RNG // (acqs * turns)
    first = lax.axis_index("pulse") * pulses_dev
    counts = jnp.stack([pulse_counts[0], first.astype(jnp.int32)])
    rate = lax.dynamic_slice(azimuth_rate, (lax.axis_index("acq") * rows,), (rows,))
    x, filt = compress_call(
        echoes, jnp.repeat(chirp_phase, 2)[None], rate[:, None], counts, acqs * turns,
        pulses_dev * turns,
    )
    real, imag = focus_call(x, filt, partner_bits[0], acqs)
    return (real[None], imag[None])


def solution(mesh):
    in_specs = (P("acq", None, "pulse", None), P(), P("acq"), P("pulse"), P("acq", None))
    out_specs = (P("acq", None, "pulse", None), P("acq", None, "pulse", None))
    devices = mesh.shape["acq"] * mesh.shape["pulse"]
    joint = RNG % (16 * devices) == 0
    return jax.shard_map(
        per_device_joint if joint else per_device,
        mesh=mesh, in_specs=in_specs, out_specs=out_specs, check_vma=False,
    )
```

```python
import functools
import math

import jax
import jax.numpy as jnp
import numpy as np
from jax import lax
from jax.experimental import pallas as pl
from jax.experimental.pallas import tpu as pltpu
from jax.sharding import PartitionSpec as P

RNG = 512
TAPS = 1024
LOOK_RNG = 4
LOOK_AZ = 16


def partner_2(shard, axis, bit):
    return lax.ppermute(shard, axis, [(i, i ^ 1 << bit) for i in range(lax.axis_size(axis))])


def part_tables(length, inverse):
    steps = jnp.arange(length, dtype=jnp.int32)
    angle = 2.0 * jnp.pi * (steps[:, None] * steps[None, :] % length).astype(jnp.float32) / length
    cosine = jnp.cos(angle)
    sine = jnp.sin(angle)
    if inverse:
        sine = -sine
    return jnp.stack([jnp.stack([cosine, -sine]), jnp.stack([sine, cosine])])


def complex_product(left_re, left_im, right_re, right_im):
    return (left_re * right_re - left_im * right_im, left_re * right_im + left_im * right_re)


def compress(echoes, toeplitz, first_pulse, live_pulses, block_cols, window):
    pulse_rows = echoes.shape[1]
    parts_re = []
    parts_im = []
    for start in range(0, RNG, block_cols):
        segment = echoes[:, :, start : start + window]
        stacked = jnp.concatenate([segment[0], segment[1]], axis=1)
        result = lax.dot_general(
            toeplitz, stacked, (((1,), (1,)), ((), ())), preferred_element_type=jnp.float32
        )
        parts_re.append(result[:block_cols])
        parts_im.append(result[block_cols:])
    joined = jnp.stack([jnp.concatenate(parts_re, axis=0), jnp.concatenate(parts_im, axis=0)])
    pulse_ids = first_pulse + jnp.arange(pulse_rows, dtype=jnp.int32)
    keep = (pulse_ids < live_pulses).astype(jnp.float32)
    return (joined * keep[None, None, :]).astype(jnp.bfloat16)


def azimuth(turned, azimuth_rate):
    columns = turned.shape[1]
    length = turned.shape[2]
    outer_len = 64
    inner_len = length // outer_len
    highest = lax.Precision.HIGHEST
    signal = turned.astype(jnp.float32).reshape(2, columns, outer_len, inner_len)
    section_one = jnp.einsum(
        "pcab,pqak->qckb", signal, part_tables(outer_len, False), precision=highest
    )
    outer_ids = jnp.arange(outer_len, dtype=jnp.int32)
    inner_ids = jnp.arange(inner_len, dtype=jnp.int32)
    twist = (
        2.0
        * jnp.pi
        * (outer_ids[:, None] * inner_ids[None, :] % length).astype(jnp.float32)
        / length
    )
    twist_cos = jnp.cos(twist)
    twist_sin = jnp.sin(twist)
    turned_re, turned_im = complex_product(section_one[0], section_one[1], twist_cos, -twist_sin)
    spectrum = jnp.einsum(
        "pckb,pqbm->qckm",
        jnp.stack([turned_re, turned_im]),
        part_tables(inner_len, False),
        precision=highest,
    )
    freq_index = outer_ids[:, None] + outer_len * inner_ids[None, :]
    signed = jnp.where(freq_index < length // 2, freq_index, freq_index - length).astype(
        jnp.float32
    )
    quad = signed * signed / length
    phase = (jnp.pi * azimuth_rate)[:, None, None] * quad[None, :, :]
    filt_re, filt_im = complex_product(spectrum[0], spectrum[1], jnp.cos(phase), -jnp.sin(phase))
    back_one = jnp.einsum(
        "pckm,pqmb->qckb",
        jnp.stack([filt_re, filt_im]),
        part_tables(inner_len, True),
        precision=highest,
    )
    undo_re, undo_im = complex_product(back_one[0], back_one[1], twist_cos, twist_sin)
    restored = jnp.einsum(
        "pckb,pqka->qcab",
        jnp.stack([undo_re, undo_im]),
        part_tables(outer_len, True),
        precision=highest,
    )
    return (restored / length).reshape(2, columns, length)


def multilook(values):
    columns = values.shape[0]
    pulse_len = values.shape[1]
    shaped = values.reshape(columns // LOOK_RNG, LOOK_RNG, pulse_len // LOOK_AZ, LOOK_AZ)
    return jnp.mean(shaped, axis=(1, 3))


def cross_looks(own_block, partner):
    own_f = own_block.astype(jnp.float32)
    other_f = partner.astype(jnp.float32)
    prod_re = own_f[0] * other_f[0] + own_f[1] * other_f[1]
    prod_im = own_f[1] * other_f[0] - own_f[0] * other_f[1]
    return jnp.stack([multilook(prod_re), multilook(prod_im)])


def per_device(raw_echo, chirp_phase, pulse_counts, azimuth_rate, partner_bits):
    echoes = raw_echo[0]
    pulses_dev = echoes.shape[1]
    block_cols = min(256, RNG)
    window = block_cols + TAPS - 1
    amplitude = 2.0 / math.sqrt(TAPS)
    table_re = (amplitude * jnp.cos(chirp_phase)).astype(jnp.bfloat16)
    table_im = (amplitude * jnp.sin(chirp_phase)).astype(jnp.bfloat16)
    padding = jnp.zeros((block_cols,), jnp.bfloat16)
    band_re = jnp.tile(jnp.concatenate([table_re, padding]), block_cols)[
        : block_cols * window
    ].reshape(block_cols, window)
    band_im = jnp.tile(jnp.concatenate([table_im, padding]), block_cols)[
        : block_cols * window
    ].reshape(block_cols, window)
    toeplitz = jnp.concatenate(
        [jnp.concatenate([band_re, band_im], axis=1), jnp.concatenate([-band_im, band_re], axis=1)],
        axis=0,
    )
    live_pulses = pulse_counts[0]
    first_pulse = lax.axis_index("pulse") * pulses_dev
    compressed = compress(echoes, toeplitz, first_pulse, live_pulses, block_cols, window)
    turned = lax.all_to_all(compressed, "pulse", split_axis=1, concat_axis=2, tiled=True)
    focused = azimuth(turned, azimuth_rate).astype(jnp.bfloat16)
    chosen = partner_bits[0]
    bit_count = lax.axis_size("acq").bit_length() - 1
    arrived = [partner_2(focused, "acq", which) for which in range(bit_count)]
    results = []
    for slot in range(2):
        partner = arrived[0]
        for which in range(1, bit_count):
            partner = jnp.where(chosen[slot] == which, arrived[which], partner)
        results.append(cross_looks(focused, partner))
    interfere_real = jnp.stack([item[0] for item in results])[None]
    interfere_imag = jnp.stack([item[1] for item in results])[None]
    return (interfere_real, interfere_imag)


OUTER = 16


def butterflies(values, sign):
    count = len(values)
    if count == 1:
        return values
    even = butterflies(values[0::2], sign)
    odd = butterflies(values[1::2], sign)
    low, high = [], []
    for k in range(count // 2):
        e_re, e_im = even[k]
        o_re, o_im = odd[k]
        if k == 0:
            t_re, t_im = o_re, o_im
        elif 4 * k == count:
            t_re, t_im = (-o_im, o_re) if sign > 0 else (o_im, -o_re)
        else:
            c = math.cos(2.0 * math.pi * k / count)
            s = sign * math.sin(2.0 * math.pi * k / count)
            t_re, t_im = o_re * c - o_im * s, o_re * s + o_im * c
        low.append((e_re + t_re, e_im + t_im))
        high.append((e_re - t_re, e_im - t_im))
    return low + high


def compress_kernel(
    block_cols, counts_ref, phase_ref, rate_ref, echo_ref, turned_ref, filt_ref, band, ready, send_sem, recv_sem,
    own_sem,
):
    step = pl.program_id(0)
    steps = pl.num_programs(0)
    acqs = lax.axis_size("acq")
    devices = acqs * lax.axis_size("pulse")
    me = lax.axis_index("pulse") * acqs + lax.axis_index("acq")
    barrier = pltpu.get_barrier_semaphore()

    def place(d):
        peer = me ^ d
        return peer, (peer % acqs, peer // acqs)

    @pl.when(step == 0)
    def _():
        def greet(d, carry):
            pl.semaphore_signal(
                barrier, inc=1, device_id=place(d)[1], device_id_type=pl.DeviceIdType.MESH
            )
            return carry

        lax.fori_loop(1, devices, greet, 0)

    pulses = echo_ref.shape[2]
    width = band.shape[2]
    window = block_cols + TAPS - 1

    @pl.when(step == 0)
    def _():
        amplitude = 2.0 / math.sqrt(TAPS)
        phase = phase_ref[...]
        cosine, sine = amplitude * jnp.cos(phase), amplitude * jnp.sin(phase)
        even = lax.broadcasted_iota(jnp.int32, phase.shape, 1) % 2 == 0
        for part, table in enumerate(
            (jnp.where(even, cosine, sine), jnp.where(even, -sine, cosine))
        ):
            row = jnp.concatenate(
                [table, jnp.zeros((1, width - 2 * TAPS), jnp.float32)], axis=1
            )
            rows = jnp.broadcast_to(row, (block_cols, width))
            band[part] = pltpu.roll(rows, 0, 1, stride=2, stride_axis=0).astype(jnp.bfloat16)

    first = counts_ref[1] + step * pulses
    ids = first + lax.broadcasted_iota(jnp.int32, (1, pulses), 1)
    keep = ids < counts_ref[0]
    per = ready.shape[3]
    slabs = block_cols // per
    for block in range(RNG // block_cols):
        echo = echo_ref[pl.ds(block * block_cols, window)].reshape(2 * window, pulses)
        for part in range(2):
            y = jnp.dot(
                band[part, :, : 2 * window], echo, preferred_element_type=jnp.float32
            )
            kept = jnp.where(keep, y, 0.0).astype(jnp.bfloat16)
            ready[step, pl.ds(block * slabs, slabs), part] = kept.reshape(slabs, per, pulses)

    @pl.when(step == 0)
    def _():
        pl.semaphore_wait(barrier, devices - 1)

    def remote(at, d):
        peer, where = place(d)
        lanes = pl.ds(pl.multiple_of(at * pulses, 128), pulses)
        return pltpu.make_async_remote_copy(
            src_ref=ready.at[at, peer],
            dst_ref=turned_ref.at[me, :, :, lanes],
            send_sem=send_sem.at[at, d],
            recv_sem=recv_sem.at[at, d],
            device_id=where,
            device_id_type=pl.DeviceIdType.MESH,
        )

    def own(at):
        lanes = pl.ds(pl.multiple_of(at * pulses, 128), pulses)
        return pltpu.make_async_copy(
            ready.at[at, me], turned_ref.at[me, :, :, lanes], own_sem.at[at]
        )

    half = devices // 2

    def send(i, carry):
        remote(step, devices - 1 - i).start()
        remote(step, half - 1 - i).start()
        return carry

    lax.fori_loop(0, half - 1, send, 0)
    remote(step, half).start()
    own(step).start()

    @pl.when(step == steps - 1)
    def _():
        outer, rows, inner = filt_ref.shape[1:]
        length = outer * inner
        rate = jnp.pi * rate_ref[...]

        def matched(k, carry):
            index = k + outer * lax.broadcasted_iota(jnp.int32, (1, inner), 1)
            signed = jnp.where(index < length // 2, index, index - length).astype(jnp.float32)
            phase = rate * (signed * signed / length)
            filt_ref[0, k] = jnp.cos(phase) / length
            filt_ref[1, k] = -jnp.sin(phase) / length
            return carry

        lax.fori_loop(0, outer, matched, 0)

        def finish(i, carry):
            remote(i // (devices - 1), i % (devices - 1) + 1).wait()
            return carry

        lax.fori_loop(0, steps * (devices - 1), finish, 0)
        for at in range(ready.shape[0]):
            own(at).wait()


def compress_call(echoes, phase, rate, counts, devices, length):
    pulses = echoes.shape[2]
    step = min(256, pulses)
    steps = pulses // step
    block_cols = 256
    width = -(-2 * (block_cols + TAPS - 1) // 128) * 128
    per = RNG // devices
    return pl.pallas_call(
        functools.partial(compress_kernel, block_cols),
        grid=(steps,),
        out_shape=(
            jax.ShapeDtypeStruct((devices, 2, per, pulses), jnp.bfloat16),
            jax.ShapeDtypeStruct((2, OUTER, per, length // OUTER), jnp.float32),
        ),
        in_specs=[
            pl.BlockSpec(memory_space=pltpu.SMEM),
            pl.BlockSpec((1, 2 * TAPS), lambda i: (0, 0)),
            pl.BlockSpec((per, 1), lambda i: (0, 0)),
            pl.BlockSpec((echoes.shape[0], 2, step), lambda i: (0, 0, i)),
        ],
        out_specs=(
            pl.BlockSpec(memory_space=pl.ANY),
            pl.BlockSpec((2, OUTER, per, length // OUTER), lambda i: (0, 0, 0, 0)),
        ),
        scratch_shapes=[
            pltpu.VMEM((2, block_cols, width), jnp.bfloat16),
            pltpu.VMEM((steps, devices, 2, per, step), jnp.bfloat16),
            pltpu.SemaphoreType.DMA((steps, devices)),
            pltpu.SemaphoreType.DMA((steps, devices)),
            pltpu.SemaphoreType.DMA((steps,)),
        ],
        compiler_params=pltpu.CompilerParams(
            vmem_limit_bytes=49 * 2**20, collective_id=0, has_side_effects=True
        ),
        name="compress",
    )(counts, phase, rate, echoes)


def focus_kernel(
    acqs, pairs, chosen_ref, x_ref, filt_ref, twist_ref, fwd_ref, inv_ref, pool_ref, look_ref,
    real_ref, imag_ref, held, image, prods, stage, landed, send_sem, recv_sem, own_sem,
):
    me = lax.axis_index("acq")
    pulse = lax.axis_index("pulse")
    barrier = pltpu.get_barrier_semaphore()
    for d in range(1, acqs):
        pl.semaphore_signal(
            barrier, inc=1, device_id=(me ^ d, pulse), device_id_type=pl.DeviceIdType.MESH
        )
    rows = x_ref.shape[2]
    local = x_ref.shape[3]
    inner = twist_ref.shape[2]
    per_src = local // inner
    chunk = 128

    def forward(index, carry):
        acq, at = index // (inner // chunk), index % (inner // chunk)
        values = []
        for a in range(OUTER):
            src = (a // per_src) * acqs + acq
            lane = pl.multiple_of((a % per_src) * inner + at * chunk, chunk)
            values.append(
                tuple(
                    x_ref[src, part, :, pl.ds(lane, chunk)].astype(jnp.float32)
                    for part in range(2)
                )
            )
        lane = pl.multiple_of(at * chunk, chunk)
        for k, (re, im) in enumerate(butterflies(values, -1)):
            c = twist_ref[0, pl.ds(k, 1), pl.ds(lane, chunk)]
            s = twist_ref[1, pl.ds(k, 1), pl.ds(lane, chunk)]
            held[acq, k, :, pl.ds(lane, chunk)] = (re * c + im * s).astype(jnp.bfloat16)
            lane_im = pl.multiple_of(lane + inner, chunk)
            held[acq, k, :, pl.ds(lane_im, chunk)] = (im * c - re * s).astype(jnp.bfloat16)
        return carry

    def middle(acq, carry):
        spec = jnp.dot(
            held[acq].reshape(OUTER * rows, 2 * inner),
            fwd_ref[...],
            preferred_element_type=jnp.float32,
        )
        s_re, s_im = spec[:, :inner], spec[:, inner:]
        f_re = filt_ref[0].reshape(OUTER * rows, inner)
        f_im = filt_ref[1].reshape(OUTER * rows, inner)
        m_re = (s_re * f_re - s_im * f_im).astype(jnp.bfloat16)
        m_im = (s_re * f_im + s_im * f_re).astype(jnp.bfloat16)
        back = jnp.dot(
            jnp.concatenate([m_re, m_im], axis=1), inv_ref[...],
            preferred_element_type=jnp.float32,
        )
        image[acq] = back.reshape(OUTER, rows, 2 * inner)
        return carry

    def inverse(index, carry):
        acq, at = index // (inner // chunk), index % (inner // chunk)
        lane = pl.multiple_of(at * chunk, chunk)
        lane_im = pl.multiple_of(lane + inner, chunk)
        values = []
        for k in range(OUTER):
            re = image[acq, k, :, pl.ds(lane, chunk)]
            im = image[acq, k, :, pl.ds(lane_im, chunk)]
            c = twist_ref[0, pl.ds(k, 1), pl.ds(lane, chunk)]
            s = twist_ref[1, pl.ds(k, 1), pl.ds(lane, chunk)]
            values.append((re * c - im * s, im * c + re * s))
        for a, (re, im) in enumerate(butterflies(values, 1)):
            image[acq, a, :, pl.ds(lane, chunk)] = re
            image[acq, a, :, pl.ds(lane_im, chunk)] = im
        return carry

    lax.fori_loop(0, acqs * (inner // chunk), forward, 0)
    lax.fori_loop(0, acqs, middle, 0)
    lax.fori_loop(0, acqs * (inner // chunk), inverse, 0)

    group = pool_ref.shape[0] // inner
    count = len(pairs) * rows
    parts = [[], []]
    for g in range(OUTER // group):
        for step in range(group):
            a = g * group + step
            lanes = pl.ds(step * inner, inner)
            for n, (one, two) in enumerate(pairs):
                o_re, o_im = image[one, a, :, :inner], image[one, a, :, inner:]
                t_re, t_im = image[two, a, :, :inner], image[two, a, :, inner:]
                for part, p in enumerate(
                    (o_re * t_re + o_im * t_im, o_im * t_re - o_re * t_im)
                ):
                    top = p.astype(jnp.bfloat16)
                    rest = (p - top.astype(jnp.float32)).astype(jnp.bfloat16)
                    at = part * count + n * rows
                    prods[pl.ds(at, rows), lanes] = top
                    prods[pl.ds(2 * count + at, rows), lanes] = rest
        z = jnp.dot(prods[...], pool_ref[...], preferred_element_type=jnp.float32)
        z = z[: 2 * count] + z[2 * count :]
        parts[0].append(z[:count])
        parts[1].append(z[count:])
    for part in range(2):
        result = jnp.dot(
            look_ref[part], jnp.concatenate(parts[part], axis=1),
            preferred_element_type=jnp.float32, precision=lax.Precision.HIGHEST,
        )
        span = result.shape[0] // acqs
        for acq in range(acqs):
            stage[acq, part] = result[acq * span : (acq + 1) * span]

    pl.semaphore_wait(barrier, acqs - 1)
    copies = [
        pltpu.make_async_remote_copy(
            src_ref=stage.at[me ^ d], dst_ref=landed.at[me],
            send_sem=send_sem.at[d], recv_sem=recv_sem.at[d],
            device_id=(me ^ d, pulse), device_id_type=pl.DeviceIdType.MESH,
        )
        for d in range(1, acqs)
    ]
    copies.append(pltpu.make_async_copy(stage.at[me], landed.at[me], own_sem))
    for copy in copies:
        copy.start()
    for copy in copies:
        copy.wait()
    bits = acqs.bit_length() - 1
    looks = rows // LOOK_RNG
    for part, ref in enumerate((real_ref, imag_ref)):
        for slot in range(2):
            bit = chosen_ref[slot]
            blocks = []
            for src in range(acqs):
                block = landed[src, part]
                taken = block[:looks]
                for which in range(1, bits):
                    taken = jnp.where(
                        bit == which, block[which * looks : (which + 1) * looks], taken
                    )
                blocks.append(taken)
            ref[slot] = jnp.concatenate(blocks, axis=0)


def focus_tables(acqs, rows, length):
    inner = length // OUTER
    b = np.arange(inner)
    angle = 2.0 * np.pi * (b[:, None] * b[None, :] % inner) / inner
    c, s = np.cos(angle), np.sin(angle)
    fwd = np.block([[c, -s], [s, c]]).astype(jnp.bfloat16)
    inv = np.block([[c, s], [-s, c]]).astype(jnp.bfloat16)
    angle = 2.0 * np.pi * (np.arange(OUTER)[:, None] * b[None, :]) / length
    twist = np.stack([np.cos(angle), np.sin(angle)]).astype(np.float32)
    span = 128 * LOOK_AZ
    pool = (np.arange(span)[:, None] // LOOK_AZ == np.arange(128)[None, :]).astype(jnp.bfloat16)
    bits = acqs.bit_length() - 1
    pairs = [(a, a ^ 1 << bit) for bit in range(bits) for a in range(acqs) if not a >> bit & 1]
    looks = rows // LOOK_RNG
    look = np.zeros((2, acqs, bits, looks, len(pairs), rows), np.float32)
    scale = 1.0 / (LOOK_RNG * LOOK_AZ)
    for n, (one, two) in enumerate(pairs):
        bit = (one ^ two).bit_length() - 1
        for r in range(rows):
            l = r // LOOK_RNG
            look[:, one, bit, l, n, r] = scale
            look[0, two, bit, l, n, r] = scale
            look[1, two, bit, l, n, r] = -scale
    look = look.reshape(2, acqs * bits * looks, len(pairs) * rows)
    return pairs, twist, fwd, inv, pool, look


def focus_call(x, filt, chosen, acqs):
    rows, local = x.shape[2], x.shape[3]
    length = x.shape[0] // acqs * local
    inner = length // OUTER
    pairs, twist, fwd, inv, pool, look = focus_tables(acqs, rows, length)
    return pl.pallas_call(
        functools.partial(focus_kernel, acqs, pairs),
        out_shape=(
            jax.ShapeDtypeStruct((2, acqs * rows // LOOK_RNG, length // LOOK_AZ), jnp.float32),
        ) * 2,
        in_specs=[pl.BlockSpec(memory_space=pltpu.SMEM)]
        + [pl.BlockSpec(memory_space=pltpu.VMEM)] * 7,
        out_specs=(pl.BlockSpec(memory_space=pltpu.VMEM),) * 2,
        scratch_shapes=[
            pltpu.VMEM((acqs, OUTER, rows, 2 * inner), jnp.bfloat16),
            pltpu.VMEM((acqs, OUTER, rows, 2 * inner), jnp.float32),
            pltpu.VMEM((4 * len(pairs) * rows, pool.shape[0]), jnp.bfloat16),
            pltpu.VMEM((acqs, 2, look.shape[1] // acqs, length // LOOK_AZ), jnp.float32),
            pltpu.VMEM((acqs, 2, look.shape[1] // acqs, length // LOOK_AZ), jnp.float32),
            pltpu.SemaphoreType.DMA((acqs,)),
            pltpu.SemaphoreType.DMA((acqs,)),
            pltpu.SemaphoreType.DMA,
        ],
        compiler_params=pltpu.CompilerParams(
            vmem_limit_bytes=48 * 2**20, collective_id=1, has_side_effects=True
        ),
        name="focus",
    )(chosen, x, filt, jnp.asarray(twist), jnp.asarray(fwd), jnp.asarray(inv), jnp.asarray(pool),
      jnp.asarray(look))


def per_device_joint(raw_echo, chirp_phase, pulse_counts, azimuth_rate, partner_bits):
    echoes = raw_echo[0].transpose(2, 0, 1)
    pulses_dev = echoes.shape[2]
    acqs, turns = lax.axis_size("acq"), lax.axis_size("pulse")
    rows = RNG // (acqs * turns)
    first = lax.axis_index("pulse") * pulses_dev
    counts = jnp.stack([pulse_counts[0], first.astype(jnp.int32)])
    rate = lax.dynamic_slice(azimuth_rate, (lax.axis_index("acq") * rows,), (rows,))
    x, filt = compress_call(
        echoes, jnp.repeat(chirp_phase, 2)[None], rate[:, None], counts, acqs * turns,
        pulses_dev * turns,
    )
    real, imag = focus_call(x, filt, partner_bits[0], acqs)
    return (real[None], imag[None])


def solution(mesh):
    in_specs = (P("acq", None, "pulse", None), P(), P("acq"), P("pulse"), P("acq", None))
    out_specs = (P("acq", None, "pulse", None), P("acq", None, "pulse", None))
    devices = mesh.shape["acq"] * mesh.shape["pulse"]
    joint = RNG % (16 * devices) == 0
    return jax.shard_map(
        per_device_joint if joint else per_device,
        mesh=mesh, in_specs=in_specs, out_specs=out_specs, check_vma=False,
    )
```
